32 devices in a mesh: dp: 8 (over z, x), chan: 4 (over y, core).
Axes of the slice: x: 2, y: 2, z: 4, core: 2. Of those that a mesh axis runs over, the one named last changes fastest.
Arguments:
- tokens: bfloat16 [224, 196, 768], P('dp', None, 'chan'), may hold values from -6 to 6
- ln1_gain: float32 [768], P('chan'), may hold values from 0.5 to 1.5
- ln1_bias: float32 [768], P('chan'), may hold values from -1.5 to 1.5
- mix_in: bfloat16 [196, 384], replicated, may hold values from -0.4375 to 0.4375
- mix_in_bias: float32 [384], replicated, may hold values from -2.5 to 2.5
- mix_out: bfloat16 [384, 196], replicated, may hold values from -0.3125 to 0.3125
- mix_out_bias: float32 [196], replicated, may hold values from -1.5 to 1.5
- ln2_gain: float32 [768], replicated, may hold values from 0.5 to 1.5
- ln2_bias: float32 [768], replicated, may hold values from -1.5 to 1.5
- chan_in: bfloat16 [768, 3072], replicated, may hold values from -0.21875 to 0.21875
- chan_in_bias: float32 [3072], replicated, may hold values from -2.5 to 2.5
- chan_out: bfloat16 [3072, 768], replicated, may hold values from -0.109375 to 0.109375
- chan_out_bias: float32 [768], replicated, may hold values from -1.5 to 1.5
- skip_masks: int32 [224, 2], P('dp'), may hold values 0 or 1
- cotangent: bfloat16 [224, 196, 768], P('dp', 'chan'), may hold values from -6 to 6
Outputs:
- output: bfloat16 [224, 196, 768], P('dp', 'chan')
- input_grad: float32 [224, 196, 768], P('dp', None, 'chan')
- grad_ln1_gain: float32 [768], replicated
- grad_ln1_bias: float32 [768], replicated
- grad_mix_in: float32 [196, 384], replicated
- grad_mix_in_bias: float32 [384], replicated
- grad_mix_out: float32 [384, 196], replicated
- grad_mix_out_bias: float32 [196], replicated
- grad_ln2_gain: float32 [768], replicated
- grad_ln2_bias: float32 [768], replicated
- grad_chan_in: float32 [768, 3072], P(None, ('dp', 'chan'))
- grad_chan_in_bias: float32 [3072], replicated
- grad_chan_out: float32 [3072, 768], P(('dp', 'chan'))
- grad_chan_out_bias: float32 [768], replicated
The draws below stay inside these ranges and needn't reach their ends.
All inputs are finite; a program needn't handle non-finite values. No bound on the sum of `skip_masks` on one device may be relied on, other than what follows from the above.
Results may differ from the reference program's by a relative error of at most 0.007.
Values may be sent and summed in bfloat16 or wider, within the bound.
No kernel may reach another device: no remote copies, remote signals or barrier semaphores. Data moves between devices by JAX's collectives and lax.ppermute only.
A program may use at most 192 MiB of HBM per device.

```python
import jax
import jax.numpy as jnp
from jax import lax

D = 768
S = 196
DS = 384
DC = 3072
IMG = 28
B = 224


def set_ends(values, key, low, top_value):
    index_at = [jax.random.randint(jax.random.fold_in(key, axis), (), 0, length) for axis, length in enumerate(values.shape)]
    widest = values.shape.index(max(values.shape))
    beside = index_at[:widest] + [(index_at[widest] + 1) % values.shape[widest]] + index_at[widest + 1:]
    return values.at[tuple(index_at)].set(low).at[tuple(beside)].set(top_value)


def levels(rng, dims, split, least, top_value):
    level = 1.0
    for position, shards_of in split:
        heights = jax.random.uniform(jax.random.fold_in(jax.random.fold_in(rng, 6), position), (shards_of,), jnp.float32, least / len(split), top_value / len(split))
        level = level * jnp.repeat(jnp.exp(heights), dims[position] // shards_of).reshape((-1,) + (1,) * (len(dims) - 1 - position))
    return level


def centred(rng, shape, width, limit, shards=(), dtype=jnp.bfloat16):
    drawn = jax.random.normal(rng, shape, jnp.float32) * width
    if len(shards) > 0:
        drawn = levels(rng, shape, shards, -0.22, 0.18) * drawn
    return jnp.clip(drawn, min=-limit, max=limit).astype(dtype)


def setup_inputs(seed: int = 0) -> dict:
    key_list = jax.random.split(jax.random.key(seed), 16)
    tokens = centred(key_list[0], (B, S, D), 1.0, 6.0, ((0, 8), (2, 4)))
    ln1_gain = jnp.clip(1.0 + 0.1 * jax.random.normal(key_list[1], (D,), jnp.float32), 0.5, 1.5)
    ln1_bias = centred(key_list[2], (D,), 0.3, 1.5, ((0, 4),), jnp.float32)
    mix_in = centred(key_list[3], (S, DS), S ** -0.5, 0.4375)
    mix_in_bias = centred(key_list[4], (DS,), 0.5, 2.5, (), jnp.float32)
    mix_out = centred(key_list[5], (DS, S), DS ** -0.5, 0.3125)
    mix_out_bias = centred(key_list[6], (S,), 0.3, 1.5, (), jnp.float32)
    ln2_gain = jnp.clip(1.0 + 0.1 * jax.random.normal(key_list[7], (D,), jnp.float32), 0.5, 1.5)
    ln2_bias = centred(key_list[8], (D,), 0.3, 1.5, (), jnp.float32)
    chan_in = centred(key_list[9], (D, DC), D ** -0.5, 0.21875)
    chan_in_bias = centred(key_list[10], (DC,), 0.5, 2.5, (), jnp.float32)
    chan_out = centred(key_list[11], (DC, D), DC ** -0.5, 0.109375)
    chan_out_bias = centred(key_list[12], (D,), 0.3, 1.5, (), jnp.float32)
    skip_masks = set_ends((jax.random.randint(key_list[13], (B, 2), 0, 4) < 3).astype(jnp.int32), jax.random.fold_in(key_list[13], 1), 0, 1)
    cotangent = centred(key_list[14], (B, S, D), 1.0, 6.0, ((0, 8), (1, 4)))
    return {"tokens": tokens, "ln1_gain": ln1_gain, "ln1_bias": ln1_bias, "mix_in": mix_in, "mix_in_bias": mix_in_bias, "mix_out": mix_out, "mix_out_bias": mix_out_bias, "ln2_gain": ln2_gain, "ln2_bias": ln2_bias, "chan_in": chan_in, "chan_in_bias": chan_in_bias, "chan_out": chan_out, "chan_out_bias": chan_out_bias, "skip_masks": skip_masks, "cotangent": cotangent}


epsilon = 1e-06
highest = lax.Precision.HIGHEST

@jax.custom_vjp
def low(v):
    return lax.optimization_barrier(v.astype(jnp.bfloat16)).astype(jnp.float32)

@jax.custom_vjp
def low_back(v):
    return v

def low_keep(v):
    return (low(v), None)

def low_pass(kept, grad):
    return (grad,)

def back_keep(v):
    return (v, None)

def back_low(kept, grad):
    return (low(grad),)
low.defvjp(low_keep, low_pass)
low_back.defvjp(back_keep, back_low)

def layer_norm(values, gain, shift):
    center = lax.optimization_barrier(jnp.mean(values, -1, keepdims=True))
    offsets = values - center
    spread = lax.optimization_barrier(jnp.mean(offsets * offsets, -1, keepdims=True))
    return offsets * lax.rsqrt(spread + epsilon) * gain + shift

def forward(inputs, ln1_gain, ln1_bias, mix_in, mix_in_bias, mix_out, mix_out_bias, ln2_gain, ln2_bias, chan_in, chan_in_bias, chan_out, chan_out_bias, keep_token, keep_chan):
    mixed = low(layer_norm(inputs, ln1_gain, ln1_bias))
    token_pre = low_back(jnp.einsum('bsd,sk->bdk', mixed, low(mix_in), precision=highest) + mix_in_bias)
    token_act = low(jax.nn.gelu(token_pre, approximate=False))
    token_out = jnp.einsum('bdk,ks->bsd', token_act, low(mix_out), precision=highest) + mix_out_bias[None, :, None]
    stream = low(low_back(inputs + keep_token[:, None, None] * token_out))
    chan_inp = low(layer_norm(stream, ln2_gain, ln2_bias))
    chan_pre = low_back(jnp.einsum('bsd,df->bsf', chan_inp, low(chan_in), precision=highest) + chan_in_bias)
    chan_act = low(jax.nn.gelu(chan_pre, approximate=False))
    chan_res = jnp.einsum('bsf,fd->bsd', chan_act, low(chan_out), precision=highest) + chan_out_bias
    return stream + keep_chan[:, None, None] * chan_res

def reference(tokens, ln1_gain, ln1_bias, mix_in, mix_in_bias, mix_out, mix_out_bias, ln2_gain, ln2_bias, chan_in, chan_in_bias, chan_out, chan_out_bias, skip_masks, cotangent):
    weights = tuple((value.astype(jnp.float32) for value in (ln1_gain, ln1_bias, mix_in, mix_in_bias, mix_out, mix_out_bias, ln2_gain, ln2_bias, chan_in, chan_in_bias, chan_out, chan_out_bias)))
    group_count = tokens.shape[0] // IMG

    def step(totals, scanned):
        image_block, mask_rows, upstream = scanned
        keep_token = mask_rows[:, 0].astype(jnp.float32)
        keep_chan = mask_rows[:, 1].astype(jnp.float32)

        def apply(inputs, *params):
            return forward(inputs, *params, keep_token, keep_chan)
        result, pullback = jax.vjp(apply, image_block.astype(jnp.float32), *weights)
        all_grads = pullback(upstream.astype(jnp.float32))
        totals = tuple((total + piece for total, piece in zip(totals, all_grads[1:])))
        return (totals, (result.astype(jnp.bfloat16), all_grads[0]))
    initial = tuple((jnp.zeros_like(value) for value in weights))
    totals, (outputs, input_grads) = lax.scan(step, initial, (tokens.reshape(group_count, IMG, S, D), skip_masks.reshape(group_count, IMG, 2), cotangent.reshape(group_count, IMG, S, D)))
    return (outputs.reshape(-1, S, D), input_grads.reshape(-1, S, D), totals[0], totals[1], totals[2], totals[3], totals[4], totals[5], totals[6], totals[7], totals[8], totals[9], totals[10], totals[11])
```

```python
import functools

import jax
import jax.numpy as jnp
from jax import lax
from jax.experimental import pallas as pl
from jax.experimental.pallas import tpu as pltpu
from jax.sharding import PartitionSpec as P

F32, BF16 = jnp.float32, jnp.bfloat16
EPS = 1e-6
RSQRT2 = 0.7071067811865476
RSQRT2PI = 0.3989422804014327
MIB = 2**20
ANY = pl.BlockSpec(memory_space=pl.ANY)
SMEM = pl.BlockSpec(memory_space=pltpu.SMEM)


def nn(a, b):
    return jnp.dot(a, b, preferred_element_type=F32)


def nt(a, b):
    return lax.dot_general(a, b, (((1,), (1,)), ((), ())), preferred_element_type=F32)


def tn(a, b):
    return lax.dot_general(a, b, (((0,), (0,)), ((), ())), preferred_element_type=F32)


def gelu_pair(x):
    half = 0.5 + 0.5 * lax.erf(x * RSQRT2)
    return x * half, half + x * (RSQRT2PI * jnp.exp(-0.5 * (x * x)))


def shape(dims, dtype=F32):
    return jax.ShapeDtypeStruct(dims, dtype)


def whole(dims):
    zeros = (0,) * len(dims)
    return pl.BlockSpec(dims, lambda i: zeros)


def at(dims, first):
    rest = (0,) * (len(dims) - 1)
    return pl.BlockSpec(dims, lambda i: (first,) + rest)


def column(row, size):
    r = lax.broadcasted_iota(jnp.int32, (size, size), 0)
    c = lax.broadcasted_iota(jnp.int32, (size, size), 1)
    return jnp.sum(jnp.where(r == c, jnp.broadcast_to(row, (size, size)), 0.0), 1, keepdims=True)


def stats_kernel(tok, out):
    images, width, _ = tok.shape

    def one(b, carry):
        x = tok[b].astype(F32)
        m = jnp.sum(x, 0, keepdims=True) * (1.0 / width)
        o = x - m
        out[0, pl.ds(b, 1), :] = m
        out[1, pl.ds(b, 1), :] = jnp.sum(o * o, 0, keepdims=True)
        return carry

    lax.fori_loop(0, images, one, 0, unroll=2)


def stats_call(tok):
    images, width, patches = tok.shape
    return pl.pallas_call(
        stats_kernel,
        grid=(1,),
        in_specs=[whole(tok.shape)],
        out_specs=whole((2, images, patches)),
        out_shape=shape((2, images, patches)),
        compiler_params=pltpu.CompilerParams(vmem_limit_bytes=24 * MIB),
        name="stats",
    )(tok)


def join_stats(stats, mr, width):
    m = 0.25 * ((stats[0][0] + stats[1][0]) + (stats[2][0] + stats[3][0]))
    q = jnp.zeros_like(m)
    for s in stats:
        o = s[0] - m
        q = q + (s[1] + width * (o * o))
    mr[0] = m
    mr[1] = lax.rsqrt(q * (1.0 / (4 * width)) + EPS)


def spread_rows(dst, src, P_, PP):
    for j in range(4):
        dst[pl.ds(j * PP, P_), :] = src[pl.ds(j * P_, P_), :].astype(F32)


def picker(rows, columns, P_, PP):
    r = lax.broadcasted_iota(jnp.int32, (rows, columns), 0)
    c = lax.broadcasted_iota(jnp.int32, (rows, columns), 1)
    pick = jnp.zeros((rows, columns), F32)
    for j in range(4):
        inside = jnp.logical_and(r >= j * PP, r < j * PP + P_)
        pick = jnp.where(jnp.logical_and(inside, c == r - j * (PP - P_)), 1.0, pick)
    return pick.astype(BF16)


def token_kernel(me, keep, t0, t1, t2, t3, tok, w_in, b_in, w_outT, b_out, g1, c1,
                 act, gp, s0, s1, s2, s3,
                 mr, left, wide, biasb, gcol, mix, rhs, buf, sem, *, first, P_, PP):
    nb, width, S = tok.shape
    K = w_in.shape[1]
    join_stats((t0, t1, t2, t3), mr, width)
    gcol[0] = jnp.broadcast_to(column(g1[...], width), (width, S))
    gcol[1] = jnp.broadcast_to(column(c1[...], width), (width, S))
    wide[...] = jnp.zeros_like(wide)
    spread_rows(wide, w_outT, P_, PP)
    left[:, 0:K] = wide[...].astype(BF16)
    left[:, K:] = picker(4 * PP, left.shape[1] - K, P_, PP)
    biasb[...] = jnp.zeros_like(biasb)
    bcol = jnp.broadcast_to(column(b_out[...], S), (S, biasb.shape[1]))
    for j in range(4):
        biasb[pl.ds(j * PP, P_), :] = bcol[j * P_:(j + 1) * P_, :]
    rhs[...] = jnp.zeros_like(rhs)

    def pair(p, carry):
        for i in range(2):
            b = 2 * p + i
            raw = tok[b]
            x = raw.astype(F32)
            m = mr[0, pl.ds(first + b, 1), :]
            r = mr[1, pl.ds(first + b, 1), :]
            mix[pl.ds(i * width, width), :] = (((x - m) * r) * gcol[0] + gcol[1]).astype(BF16)
            rhs[pl.ds(i * width, width), K:K + S] = raw
        pre = nn(mix[...], w_in[...]) + b_in[...]
        g, d = gelu_pair(pre)
        k0, k1 = keep[first + 2 * p], keep[first + 2 * p + 1]
        rows = lax.broadcasted_iota(jnp.int32, (2 * width, 1), 0)
        a = (g * jnp.where(rows < width, k0, k1)).astype(BF16)
        rhs[:, 0:K] = a
        here = pl.ds(pl.multiple_of(p * 2 * width, 2 * width), 2 * width)
        act[here, :] = a
        gp[here, :] = d.astype(BF16)
        lanes = lax.broadcasted_iota(jnp.int32, (1, 2 * width), 1)
        out = nt(left[...], rhs[...]) + biasb[...] * jnp.where(lanes < width, k0, k1)
        for j in range(4):
            buf[j, p] = out[j * PP:(j + 1) * PP, :].astype(BF16)
        return carry

    lax.fori_loop(0, nb // 2, pair, 0)
    sends = (s0, s1, s2, s3)
    copies = [pltpu.make_async_copy(buf.at[me[0] ^ k], sends[k], sem.at[k]) for k in range(4)]
    for c in copies:
        c.start()
    for c in copies:
        c.wait()


def token_call(me, keep, stats, tok, w_in, b_in, w_outT, b_out, g1, c1, half, P_, PP):
    images, width, S = tok.shape
    nb = images // 2
    K = w_in.shape[1]
    piece = shape((nb // 2, PP, 2 * width), BF16)
    return pl.pallas_call(
        functools.partial(token_kernel, first=half * nb, P_=P_, PP=PP),
        grid=(1,),
        in_specs=[SMEM, SMEM] + [whole(stats[0].shape)] * 4 + [at((nb, width, S), half), whole(w_in.shape), whole(b_in.shape),
                  whole(w_outT.shape), whole(b_out.shape), whole(g1.shape), whole(c1.shape)],
        out_specs=[whole((nb * width, K)), whole((nb * width, K)), ANY, ANY, ANY, ANY],
        out_shape=[shape((nb * width, K), BF16), shape((nb * width, K), BF16), piece, piece, piece, piece],
        scratch_shapes=[pltpu.VMEM((2, images, S), F32), pltpu.VMEM((4 * PP, K + 256), BF16), pltpu.VMEM((4 * PP, K), F32),
                        pltpu.VMEM((4 * PP, 2 * width), F32), pltpu.VMEM((2, width, S), F32), pltpu.VMEM((2 * width, S), BF16),
                        pltpu.VMEM((2 * width, K + 256), BF16), pltpu.VMEM((4, nb // 2, PP, 2 * width), BF16),
                        pltpu.SemaphoreType.DMA((4,))],
        compiler_params=pltpu.CompilerParams(vmem_limit_bytes=32 * MIB),
        name="token_forward",
    )(me, keep, *stats, tok, w_in, b_in, w_outT, b_out, g1, c1)


def chan_kernel(me, keep, p0, p1, p2, p3, cot, w1, w2, b1, b2, g2, c2, *rest, nb, P_, R, RB, first, joined):
    rest = rest[1:] if joined else rest
    (act, pg, b3, x, og, out, s0, s1, s2, s3, gg, gc, b4,
     st, ct, nrm, r2s, acc_o, acc_i, bufi, bufo, sem) = rest
    step = pl.program_id(0)
    last = pl.num_programs(0) - 1
    W = x.shape[1]
    q = W // 4
    rows = nb * P_
    pieces = (p0, p1, p2, p3)
    sends = (s0, s1, s2, s3)

    @pl.when(step == 0)
    def _():
        copies = [pltpu.make_async_copy(pieces[k], bufi.at[me[0] ^ k], sem.at[k]) for k in range(4)]
        for c in copies:
            c.start()
        tail = jnp.zeros((R - rows, W), F32)
        ct[pl.ds(rows, R - rows), :] = tail
        st[pl.ds(rows, R - rows), :] = tail
        for b in range(nb):
            v = cot[b].astype(F32)
            ct[pl.ds(b * P_, P_), :] = v
            st[pl.ds(b * P_, P_), :] = v * keep[first + b]

        def put(i, s):
            r = pl.ds(pl.multiple_of(i * RB, RB), RB)
            v = st[r, :]
            og[r, :] = v.astype(BF16)
            return s + jnp.sum(v, 0, keepdims=True)

        b4[...] = lax.fori_loop(0, R // RB, put, jnp.zeros((1, W), F32))
        for c in copies:
            c.wait()
        for b in range(nb):
            lo = (b % 2) * q
            v = jnp.concatenate([bufi[j, b // 2][0:P_, lo:lo + q].astype(F32) for j in range(4)], axis=1)
            st[pl.ds(b * P_, P_), :] = v

        def norm(i, _):
            r = pl.ds(pl.multiple_of(i * RB, RB), RB)
            v = st[r, :]
            m = jnp.mean(v, 1, keepdims=True)
            o = v - m
            rr = lax.rsqrt(jnp.mean(o * o, 1, keepdims=True) + EPS)
            n = o * rr
            nrm[r, :] = n
            r2s[r, :] = jnp.broadcast_to(rr, (RB, 128))
            x[r, :] = (n * g2[...] + c2[...]).astype(BF16)
            return 0

        lax.fori_loop(0, R // RB, norm, 0)
        acc_o[...] = jnp.zeros_like(acc_o)
        acc_i[...] = jnp.zeros_like(acc_i)

    pre = nn(x[...], w1[...]) + b1[...]
    g, gp = gelu_pair(pre)
    a = g.astype(BF16)
    act[...] = a
    d = (nt(og[...], w2[...]) * gp).astype(BF16)
    pg[...] = d
    b3[...] = jnp.sum(d.astype(F32), 0, keepdims=True)
    acc_o[...] += nn(a, w2[...])
    acc_i[...] += nt(d, w1[...])

    @pl.when(step == last)
    def _():
        def back(i, s):
            r = pl.ds(pl.multiple_of(i * RB, RB), RB)
            e = acc_i[r, :]
            n = nrm[r, :]
            sg, sc = s
            sg = sg + jnp.sum((e * n).reshape(RB // 8, 8, W), 0)
            sc = sc + jnp.sum(e.reshape(RB // 8, 8, W), 0)
            e = e * g2[...]
            m1 = jnp.mean(e, 1, keepdims=True)
            m2 = jnp.mean(e * n, 1, keepdims=True)
            acc_i[r, :] = ct[r, :] + r2s[r, 0:1] * (e - m1 - n * m2)
            return sg, sc

        z = jnp.zeros((8, W), F32)
        sg, sc = lax.fori_loop(0, R // RB, back, (z, z))
        gg[...] = jnp.sum(sg, 0, keepdims=True)
        gc[...] = jnp.sum(sc, 0, keepdims=True)
        for b in range(nb):
            r = pl.ds(b * P_, P_)
            out[b] = (st[r, :] + keep[first + b] * (acc_o[r, :] + b2[...])).astype(BF16)
        for p in range(nb // 2):
            va = acc_i[pl.ds(2 * p * P_, P_), :]
            vb = acc_i[pl.ds((2 * p + 1) * P_, P_), :]
            for j in range(4):
                bufo[j, p, 0:P_, :] = jnp.concatenate([va[:, j * q:(j + 1) * q], vb[:, j * q:(j + 1) * q]], axis=1).astype(BF16)
                bufo[j, p, P_:, :] = jnp.zeros((bufo.shape[2] - P_, 2 * q), BF16)
        copies = [pltpu.make_async_copy(bufo.at[me[0] ^ k], sends[k], sem.at[k]) for k in range(4)]
        for c in copies:
            c.start()
        for c in copies:
            c.wait()


def chan_call(me, keep, pieces, cot, half, w1, w2, b1, b2, g2, c2, out_before, fb=512):
    images, P_, W = cot.shape
    nb = images // 2
    rows = nb * P_
    R = -(-rows // 16) * 16
    F = w1.shape[1]
    wide = pl.BlockSpec((R, fb), lambda i: (0, i))
    line = pl.BlockSpec((1, fb), lambda i: (0, i))
    row = whole((1, W))
    piece = shape(pieces[0].shape, BF16)
    joined = out_before is not None
    args = (me, keep, *pieces, cot, w1, w2, b1, b2, g2, c2) + ((out_before,) if joined else ())
    return pl.pallas_call(
        functools.partial(chan_kernel, nb=nb, P_=P_, R=R, RB=16, first=half * nb, joined=joined),
        grid=(F // fb,),
        in_specs=[SMEM, SMEM, ANY, ANY, ANY, ANY, at((nb, P_, W), half),
                  pl.BlockSpec((W, fb), lambda i: (0, i)), pl.BlockSpec((fb, W), lambda i: (i, 0)),
                  line, row, row, row] + ([ANY] if joined else []),
        out_specs=[wide, wide, line, whole((R, W)), whole((R, W)), at((nb, P_, W), half), ANY, ANY, ANY, ANY, row, row, row],
        out_shape=[shape((R, F), BF16), shape((R, F), BF16), shape((1, F)), shape((R, W), BF16), shape((R, W), BF16),
                   shape(cot.shape, BF16), piece, piece, piece, piece, shape((1, W)), shape((1, W)), shape((1, W))],
        scratch_shapes=[pltpu.VMEM((R, W), F32)] * 3 + [pltpu.VMEM((R, 128), F32), pltpu.VMEM((R, W), F32), pltpu.VMEM((R, W), F32),
                        pltpu.VMEM((4,) + piece.shape, BF16), pltpu.VMEM((4,) + piece.shape, BF16), pltpu.SemaphoreType.DMA((4,))],
        input_output_aliases={13: 5} if joined else {},
        compiler_params=pltpu.CompilerParams(vmem_limit_bytes=56 * MIB),
        name="channel_mlp",
    )(*args)


def grad_kernel(a0, a1, b0, b1, out):
    out[...] = (tn(a0[...], b0[...]) + tn(a1[...], b1[...])).astype(BF16)


def grad_call(a, b, fb=768):
    R, F = a[0].shape
    W = b[0].shape[1]
    wide = pl.BlockSpec((R, fb), lambda i: (0, i))
    return pl.pallas_call(
        grad_kernel,
        grid=(F // fb,),
        in_specs=[wide, wide, whole((R, W)), whole((R, W))],
        out_specs=pl.BlockSpec((fb, W), lambda i: (i, 0)),
        out_shape=shape((F, W), BF16),
        compiler_params=pltpu.CompilerParams(vmem_limit_bytes=40 * MIB),
        name="channel_grad",
    )(*a, *b)


def as_row(col, size):
    r = lax.broadcasted_iota(jnp.int32, (size, size), 0)
    c = lax.broadcasted_iota(jnp.int32, (size, size), 1)
    return jnp.sum(jnp.where(r == c, jnp.broadcast_to(col, (size, size)), 0.0), 0, keepdims=True)


def back_kernel(me, keep, t0, t1, t2, t3, p0, p1, p2, p3, act, gp, tok, w_in, w_outT, g1, c1, *rest, first, P_, PP, joined):
    if joined:
        before, rest = rest[:6], rest[6:]
    u, ps, gw1, gw2, ob1, ob2, og, oc, mr, right, wide, gcol, mix, bufi, gb1, gb2, gg, gc, sem = rest
    nb, width, S = tok.shape
    K = w_in.shape[1]
    pieces = (p0, p1, p2, p3)
    copies = [pltpu.make_async_copy(pieces[k], bufi.at[me[0] ^ k], sem.at[k]) for k in range(4)]
    for c in copies:
        c.start()
    join_stats((t0, t1, t2, t3), mr, width)
    gcol[0] = jnp.broadcast_to(column(g1[...], width), (width, S))
    gcol[1] = jnp.broadcast_to(column(c1[...], width), (width, S))
    wide[...] = jnp.zeros_like(wide)
    spread_rows(wide, w_outT, P_, PP)
    right[:, 0:K] = wide[...].astype(BF16)
    right[:, K:] = picker(4 * PP, right.shape[1] - K, P_, PP)
    for o in (gb1, gb2, gg, gc):
        o[...] = jnp.zeros_like(o)
    if joined:
        gw1[...] = before[0][...]
        gw2[...] = before[1][...]
    else:
        gw1[...] = jnp.zeros_like(gw1)
        gw2[...] = jnp.zeros_like(gw2)
    for c in copies:
        c.wait()

    def pair(p, carry):
        sg = bufi[:, p].reshape(4 * PP, 2 * width)
        here = pl.ds(pl.multiple_of(p * 2 * width, 2 * width), 2 * width)
        k0, k1 = keep[first + 2 * p], keep[first + 2 * p + 1]
        lanes = lax.broadcasted_iota(jnp.int32, (1, 2 * width), 1)
        gb2[...] += sg.astype(F32) * jnp.where(lanes < width, k0, k1)
        both = tn(sg, right[...])
        rows = lax.broadcasted_iota(jnp.int32, (2 * width, 1), 0)
        pre1 = ((both[:, 0:K] * gp[here, :].astype(F32)) * jnp.where(rows < width, k0, k1)).astype(BF16)
        gb1[...] += jnp.sum(pre1.astype(F32).reshape(2 * width // 8, 8, K), 0)
        gw2[...] += nn(sg, act[here, :])
        ng = nt(pre1, w_in[...])
        for i in range(2):
            b = 2 * p + i
            part = slice(i * width, (i + 1) * width)
            m = mr[0, pl.ds(first + b, 1), :]
            r = mr[1, pl.ds(first + b, 1), :]
            n = (tok[b].astype(F32) - m) * r
            mix[pl.ds(i * width, width), :] = (n * gcol[0] + gcol[1]).astype(BF16)
            v = ng[part, :]
            gg[...] += v * n
            gc[...] += v
            e = v * gcol[0]
            ps[0, pl.ds(b, 1), :] = jnp.sum(e, 0, keepdims=True)
            ps[1, pl.ds(b, 1), :] = jnp.sum(e * n, 0, keepdims=True)
            u[b] = both[part, K:K + S] + r * e
        gw1[...] += tn(mix[...], pre1)
        return carry

    lax.fori_loop(0, nb // 2, pair, 0)
    sums = (jnp.sum(gb1[...], 0, keepdims=True),
            as_row(jnp.sum(gb2[...], 1, keepdims=True), 4 * PP),
            as_row(jnp.sum(gg[...], 1, keepdims=True), width),
            as_row(jnp.sum(gc[...], 1, keepdims=True), width))
    for i, o in enumerate((ob1, ob2, og, oc)):
        o[...] = sums[i] + before[2 + i][...] if joined else sums[i]


def back_call(me, keep, stats, pieces, act, gp, tok, w_in, w_outT, g1, c1, half, P_, PP, before):
    images, width, S = tok.shape
    nb = images // 2
    K = w_in.shape[1]
    joined = before is not None
    sums = [(S, K), (4 * PP, K), (1, K), (1, 4 * PP), (1, width), (1, width)]
    args = (me, keep, *stats, *pieces, act, gp, tok, w_in, w_outT, g1, c1) + (tuple(before) if joined else ())
    return pl.pallas_call(
        functools.partial(back_kernel, first=half * nb, P_=P_, PP=PP, joined=joined),
        grid=(1,),
        in_specs=[SMEM, SMEM] + [whole(stats[0].shape)] * 4 + [ANY] * 4 + [whole(act.shape), whole(gp.shape),
                  at((nb, width, S), half), whole(w_in.shape), whole(w_outT.shape), whole(g1.shape), whole(c1.shape)]
                 + ([whole(s) for s in sums] if joined else []),
        out_specs=[whole((nb, width, S)), whole((2, nb, S))] + [whole(s) for s in sums],
        out_shape=[shape((nb, width, S)), shape((2, nb, S))] + [shape(s) for s in sums],
        scratch_shapes=[pltpu.VMEM((2, images, S), F32), pltpu.VMEM((4 * PP, K + 256), BF16), pltpu.VMEM((4 * PP, K), F32),
                        pltpu.VMEM((2, width, S), F32), pltpu.VMEM((2 * width, S), BF16), pltpu.VMEM((4,) + pieces[0].shape, BF16),
                        pltpu.VMEM((8, K), F32), pltpu.VMEM((4 * PP, 2 * width), F32), pltpu.VMEM((width, S), F32),
                        pltpu.VMEM((width, S), F32), pltpu.SemaphoreType.DMA((4,))],
        compiler_params=pltpu.CompilerParams(vmem_limit_bytes=48 * MIB),
        name="token_backward",
    )(*args)


def finish_kernel(t0, t1, t2, t3, s0, s1, s2, s3, u, tok, *rest, first, joined):
    out, mr = rest[1:] if joined else rest
    nb, width, S = tok.shape
    join_stats((t0, t1, t2, t3), mr, width)
    scale = 1.0 / (4 * width)

    def one(b, carry):
        a = ((s0[0, pl.ds(b, 1), :] + s1[0, pl.ds(b, 1), :]) + (s2[0, pl.ds(b, 1), :] + s3[0, pl.ds(b, 1), :])) * scale
        c = ((s0[1, pl.ds(b, 1), :] + s1[1, pl.ds(b, 1), :]) + (s2[1, pl.ds(b, 1), :] + s3[1, pl.ds(b, 1), :])) * scale
        m = mr[0, pl.ds(first + b, 1), :]
        r = mr[1, pl.ds(first + b, 1), :]
        n = (tok[b].astype(F32) - m) * r
        out[b] = u[b] - r * (a + n * c)
        return carry

    lax.fori_loop(0, nb, one, 0, unroll=2)


def finish_call(stats, sums, u, tok, half, out_before):
    images, width, S = tok.shape
    nb = images // 2
    joined = out_before is not None
    return pl.pallas_call(
        functools.partial(finish_kernel, first=half * nb, joined=joined),
        grid=(1,),
        in_specs=[whole(stats[0].shape)] * 4 + [whole(sums[0].shape)] * 4 + [whole(u.shape), at((nb, width, S), half)]
                 + ([ANY] if joined else []),
        out_specs=at((nb, width, S), half),
        out_shape=shape((images, width, S)),
        scratch_shapes=[pltpu.VMEM((2, images, S), F32)],
        input_output_aliases={10: 0} if joined else {},
        compiler_params=pltpu.CompilerParams(vmem_limit_bytes=40 * MIB),
        name="norm_backward",
    )(*stats, *sums, u, tok, *((out_before,) if joined else ()))


def exchange(value):
    return [value] + [lax.ppermute(value, "chan", [(i, i ^ k) for i in range(4)]) for k in (1, 2, 3)]


def trade(pieces):
    return [pieces[0]] + [lax.ppermute(pieces[k], "chan", [(i, i ^ k) for i in range(4)]) for k in (1, 2, 3)]


def shards(tokens, ln1_gain, ln1_bias, mix_in, mix_in_bias, mix_out, mix_out_bias, ln2_gain, ln2_bias,
           chan_in, chan_in_bias, chan_out, chan_out_bias, skip_masks, cotangent):
    images, S, width = tokens.shape
    P_ = cotangent.shape[1]
    W = cotangent.shape[2]
    PP = -(-P_ // 8) * 8
    tok = jnp.swapaxes(tokens, 1, 2)
    w_outT = jnp.swapaxes(mix_out, 0, 1)
    row = lambda v: v.reshape(1, -1)
    chan = lax.axis_index("chan")
    me = chan.reshape(1).astype(jnp.int32)
    keep1 = skip_masks[:, 0].astype(F32)
    keep2 = skip_masks[:, 1].astype(F32)
    g1, c1 = row(ln1_gain), row(ln1_bias)

    stats = exchange(stats_call(tok))
    halves = (0, 1)
    fwd = [token_call(me, keep1, stats, tok, mix_in, row(mix_in_bias), w_outT, row(mix_out_bias), g1, c1, h, P_, PP) for h in halves]
    arrived = [trade(f[2:6]) for f in fwd]
    chans, out = [], None
    for h in halves:
        r = chan_call(me, keep2, arrived[h], cotangent, h, chan_in, chan_out, row(chan_in_bias), row(chan_out_bias),
                      row(ln2_gain), row(ln2_bias), out)
        out = r[5]
        chans.append(r)
    returned = [trade(r[6:10]) for r in chans]
    grad_w4 = grad_call([r[0] for r in chans], [r[4] for r in chans])
    grad_w3 = grad_call([r[1] for r in chans], [r[3] for r in chans])
    sums, back = None, []
    for h in halves:
        r = back_call(me, keep1, stats, returned[h], fwd[h][0], fwd[h][1], tok, mix_in, w_outT, g1, c1, h, P_, PP, sums)
        sums = r[2:]
        back.append(r)
    grad = None
    for h in halves:
        grad = finish_call(stats, exchange(back[h][1]), back[h][0], tok, h, grad)
    gw1, gw2, gb1, gb2, gg1, gc1 = sums
    place = lambda v: lax.dynamic_update_slice(jnp.zeros((W,), F32), v.reshape(-1), (chan * width,))
    unpad = lambda v: v.reshape(4, PP, -1)[:, :P_].reshape(S, -1)
    both = lambda i: (chans[0][i] + chans[1][i]).reshape(-1)
    small = lax.psum((place(gg1), place(gc1), gw1, gb1.reshape(-1), unpad(gw2), unpad(gb2.reshape(-1, 1)).reshape(-1),
                      both(10), both(11), both(2), both(12)), ("dp", "chan"))
    s_g1, s_c1, s_w1, s_b1, s_w2, s_b2, s_g2, s_c2, s_b3, s_b4 = small
    share_w4 = lax.psum_scatter(grad_w4, ("dp", "chan"), scatter_dimension=0, tiled=True).astype(F32)
    share_w3 = lax.psum_scatter(grad_w3, ("dp", "chan"), scatter_dimension=0, tiled=True).astype(F32)
    return (out, jnp.swapaxes(grad, 1, 2), s_g1, s_c1, s_w1, s_b1, jnp.swapaxes(s_w2, 0, 1), s_b2, s_g2, s_c2,
            jnp.swapaxes(share_w3, 0, 1), s_b3, share_w4, s_b4)


def solution(mesh):
    rep = P()
    return jax.shard_map(
        shards, mesh=mesh,
        in_specs=(P("dp", None, "chan"), P("chan"), P("chan")) + (rep,) * 10 + (P("dp", None), P("dp", "chan", None)),
        out_specs=(P("dp", "chan", None), P("dp", None, "chan"), rep, rep, rep, rep, rep, rep, rep, rep,
                   P(None, ("dp", "chan")), rep, P(("dp", "chan"), None), rep),
        check_vma=False,
    )
```

```python
import functools

import jax
import jax.numpy as jnp
from jax import lax
from jax.experimental import pallas as pl
from jax.experimental.pallas import tpu as pltpu
from jax.sharding import PartitionSpec as P

F32, BF16 = jnp.float32, jnp.bfloat16
EPS = 1e-6
RSQRT2 = 0.7071067811865476
RSQRT2PI = 0.3989422804014327
LIMIT = 60 * 2**20
ANY = pl.BlockSpec(memory_space=pl.ANY)
SMEM = pl.BlockSpec(memory_space=pltpu.SMEM)


def nn(a, b):
    return jnp.dot(a, b, preferred_element_type=F32)


def nt(a, b):
    return lax.dot_general(a, b, (((1,), (1,)), ((), ())), preferred_element_type=F32)


def tn(a, b):
    return lax.dot_general(a, b, (((0,), (0,)), ((), ())), preferred_element_type=F32)


def gelu_pair(x):
    half = 0.5 + 0.5 * lax.erf(x * RSQRT2)
    return x * half, half + x * (RSQRT2PI * jnp.exp(-0.5 * (x * x)))


def shape(dims, dtype=F32):
    return jax.ShapeDtypeStruct(dims, dtype)


def cost(weight):
    return pl.CostEstimate(flops=10**11 * weight + 1, bytes_accessed=1, transcendentals=0)


def whole(dims):
    zeros = (0,) * len(dims)
    return pl.BlockSpec(dims, lambda i: zeros)


def at(dims, first):
    rest = (0,) * (len(dims) - 1)
    return pl.BlockSpec(dims, lambda i: (first,) + rest)


def column(row, size):
    r = lax.broadcasted_iota(jnp.int32, (size, size), 0)
    c = lax.broadcasted_iota(jnp.int32, (size, size), 1)
    return jnp.sum(jnp.where(r == c, jnp.broadcast_to(row, (size, size)), 0.0), 1, keepdims=True)


def stats_kernel(tok, out):
    images, width, _ = tok.shape
    first = pl.program_id(0) * images
    for b in range(images):
        x = tok[b].astype(F32)
        m = jnp.sum(x, 0, keepdims=True) * (1.0 / width)
        o = x - m
        out[0, pl.ds(first + b, 1), :] = m
        out[1, pl.ds(first + b, 1), :] = jnp.sum(o * o, 0, keepdims=True)


def stats_call(tok, steps=4):
    images, width, patches = tok.shape
    return pl.pallas_call(
        stats_kernel,
        grid=(steps,),
        in_specs=[pl.BlockSpec((images // steps, width, patches), lambda i: (i, 0, 0))],
        out_specs=whole((2, images, patches)),
        out_shape=shape((2, images, patches)),
        compiler_params=pltpu.CompilerParams(vmem_limit_bytes=LIMIT),
        cost_estimate=cost(0),
        name="stats",
    )(tok)


def join_stats(stats, mr, width):
    m = 0.25 * ((stats[0][0] + stats[1][0]) + (stats[2][0] + stats[3][0]))
    q = jnp.zeros_like(m)
    for s in stats:
        o = s[0] - m
        q = q + (s[1] + width * (o * o))
    mr[0] = m
    mr[1] = lax.rsqrt(q * (1.0 / (4 * width)) + EPS)


def spread_rows(dst, src, P_, PP):
    for j in range(4):
        dst[pl.ds(j * PP, P_), :] = src[pl.ds(j * P_, P_), :].astype(F32)


def picker(rows, columns, P_, PP):
    r = lax.broadcasted_iota(jnp.int32, (rows, columns), 0)
    c = lax.broadcasted_iota(jnp.int32, (rows, columns), 1)
    pick = jnp.zeros((rows, columns), F32)
    for j in range(4):
        inside = jnp.logical_and(r >= j * PP, r < j * PP + P_)
        pick = jnp.where(jnp.logical_and(inside, c == r - j * (PP - P_)), 1.0, pick)
    return pick.astype(BF16)


def token_kernel(me, keep, t0, t1, t2, t3, tok, w_in, b_in, w_outT, b_out, g1, c1,
                 act, gp, s0, s1, s2, s3, mr, left, wide, biasb, gcol, mix, rhs, buf, *, first, P_, PP):
    _, width, S = tok.shape
    K = w_in.shape[1]
    p = pl.program_id(0)

    @pl.when(p == 0)
    def _():
        join_stats((t0, t1, t2, t3), mr, width)
        gcol[0] = jnp.broadcast_to(column(g1[...], width), (width, S))
        gcol[1] = jnp.broadcast_to(column(c1[...], width), (width, S))
        wide[...] = jnp.zeros_like(wide)
        spread_rows(wide, w_outT, P_, PP)
        left[:, 0:K] = wide[...].astype(BF16)
        left[:, K:] = picker(4 * PP, left.shape[1] - K, P_, PP)
        biasb[...] = jnp.zeros_like(biasb)
        bcol = jnp.broadcast_to(column(b_out[...], S), (S, biasb.shape[1]))
        for j in range(4):
            biasb[pl.ds(j * PP, P_), :] = bcol[j * P_:(j + 1) * P_, :]
        rhs[...] = jnp.zeros_like(rhs)

    for i in range(2):
        b = first + 2 * p + i
        raw = tok[i]
        m = mr[0, pl.ds(b, 1), :]
        r = mr[1, pl.ds(b, 1), :]
        mix[pl.ds(i * width, width), :] = (((raw.astype(F32) - m) * r) * gcol[0] + gcol[1]).astype(BF16)
        rhs[pl.ds(i * width, width), K:K + S] = raw
    g, d = gelu_pair(nn(mix[...], w_in[...]) + b_in[...])
    k0, k1 = keep[first + 2 * p], keep[first + 2 * p + 1]
    rows = lax.broadcasted_iota(jnp.int32, (2 * width, 1), 0)
    a = (g * jnp.where(rows < width, k0, k1)).astype(BF16)
    rhs[:, 0:K] = a
    act[...] = a
    gp[...] = d.astype(BF16)
    lanes = lax.broadcasted_iota(jnp.int32, (1, 2 * width), 1)
    out = nt(left[...], rhs[...]) + biasb[...] * jnp.where(lanes < width, k0, k1)
    for j in range(4):
        buf[j] = out[j * PP:(j + 1) * PP, :].astype(BF16)
    for k, o in enumerate((s0, s1, s2, s3)):
        o[0] = buf[me[1] ^ k]


def token_call(ids, keep, stats, tok, w_in, b_in, w_outT, b_out, g1, c1, half, P_, PP):
    images, width, S = tok.shape
    nb = images // 2
    K = w_in.shape[1]
    piece = shape((nb // 2, PP, 2 * width), BF16)
    rows = pl.BlockSpec((2 * width, K), lambda i: (i, 0))
    send = pl.BlockSpec((1, PP, 2 * width), lambda i: (i, 0, 0))
    return pl.pallas_call(
        functools.partial(token_kernel, first=half * nb, P_=P_, PP=PP),
        grid=(nb // 2,),
        in_specs=[SMEM, SMEM] + [whole(stats[0].shape)] * 4
                 + [pl.BlockSpec((2, width, S), lambda i: (half * (nb // 2) + i, 0, 0)), whole(w_in.shape), whole(b_in.shape),
                    whole(w_outT.shape), whole(b_out.shape), whole(g1.shape), whole(c1.shape)],
        out_specs=[rows, rows, send, send, send, send],
        out_shape=[shape((nb * width, K), BF16), shape((nb * width, K), BF16), piece, piece, piece, piece],
        scratch_shapes=[pltpu.VMEM((2, images, S), F32), pltpu.VMEM((4 * PP, K + 256), BF16), pltpu.VMEM((4 * PP, K), F32),
                        pltpu.VMEM((4 * PP, 2 * width), F32), pltpu.VMEM((2, width, S), F32), pltpu.VMEM((2 * width, S), BF16),
                        pltpu.VMEM((2 * width, K + 256), BF16), pltpu.VMEM((4, PP, 2 * width), BF16)],
        compiler_params=pltpu.CompilerParams(vmem_limit_bytes=LIMIT),
        cost_estimate=cost(half),
        name="token_forward",
    )(ids, keep, *stats, tok, w_in, b_in, w_outT, b_out, g1, c1)


def upstream_kernel(keep, cot, og, b4, packed, *, P_):
    nb = cot.shape[0]
    rows = nb * P_
    half = pl.program_id(0)

    @pl.when(half == 0)
    def _():
        b4[...] = jnp.zeros_like(b4)
        packed[pl.ds(rows, packed.shape[0] - rows), :] = jnp.zeros((packed.shape[0] - rows, packed.shape[1]), F32)

    for b in range(nb):
        packed[pl.ds(b * P_, P_), :] = cot[b].astype(F32) * keep[half * nb + b]
    v = packed[...]
    og[0] = v.astype(BF16)
    b4[...] += jnp.sum(v, 0, keepdims=True)


def upstream_call(keep, cot, R):
    images, P_, W = cot.shape
    return pl.pallas_call(
        functools.partial(upstream_kernel, P_=P_),
        grid=(2,),
        in_specs=[SMEM, pl.BlockSpec((images // 2, P_, W), lambda i: (i, 0, 0))],
        out_specs=[pl.BlockSpec((1, R, W), lambda i: (i, 0, 0)), whole((1, W))],
        out_shape=[shape((2, R, W), BF16), shape((1, W))],
        scratch_shapes=[pltpu.VMEM((R, W), F32)],
        compiler_params=pltpu.CompilerParams(vmem_limit_bytes=LIMIT),
        cost_estimate=cost(0),
        name="upstream",
    )(keep, cot)


def chan_kernel(*refs, nb, P_, R, half, dp, blk):
    (ids, keep2, p0, p1, p2, p3, cot, og, w1, w2, b1, b2, g2, c2), refs = refs[:14], refs[14:]
    if half:
        (before4, before3, _, keep4, send4, keep3, send3), refs = refs[:7], refs[7:]
    else:
        (grad4, grad3), refs = refs[:2], refs[2:]
    (b3, out, s0, s1, s2, s3, gg, gc, x, nrm, r2s, acc_o, acc_i, bufi, bufo, ct, ct_sem), refs = refs[:17], refs[17:]
    step = pl.program_id(0)
    last = pl.num_programs(0) - 1
    W = x.shape[1]
    fb = w1.shape[1]
    q = W // 4
    PP = bufi.shape[2]
    load_ct = pltpu.make_async_copy(cot.at[pl.ds(half * nb, nb)], ct, ct_sem)
    if half:
        old4, old3, old_sem = refs
        here = pl.ds(step * fb, fb)
        load4 = pltpu.make_async_copy(before4.at[here], old4, old_sem.at[0])
        load3 = pltpu.make_async_copy(before3.at[here], old3, old_sem.at[1])
        load4.start()
        load3.start()

    @pl.when(step == 0)
    def _():
        load_ct.start()
        for k, p in enumerate((p0, p1, p2, p3)):
            bufi[ids[1] ^ k] = p[...]
        for b in range(nb):
            lo = (b % 2) * q
            v = jnp.concatenate([bufi[j, b // 2][:, lo:lo + q].astype(F32) for j in range(4)], axis=1)
            o = v - jnp.mean(v, 1, keepdims=True)
            rr = lax.rsqrt(jnp.mean(o * o, 1, keepdims=True) + EPS)
            n = o * rr
            nrm[b] = n
            r2s[b] = jnp.broadcast_to(rr, (PP, 128))
            acc_i[pl.ds(b * P_, PP), :] = n * g2[...] + c2[...]
        x[...] = acc_i[0:R, :].astype(BF16)
        acc_i[...] = jnp.zeros_like(acc_i)
        acc_o[...] = jnp.broadcast_to(b2[...], acc_o.shape)

    g, gp = gelu_pair(nn(x[...], w1[...]) + b1[...])
    a = g.astype(BF16)
    d = (nt(og[0], w2[...]) * gp).astype(BF16)
    b3[...] = jnp.sum(d.astype(F32), 0, keepdims=True)
    acc_o[...] += nn(a, w2[...])
    acc_i[0:R, :] += nt(d, w1[...])
    if half:
        load4.wait()
        load3.wait()
        core = ids[1] & 1
        per = fb // (4 * blk)
        for total, mine, other in ((tn(a, og[0]) + old4[...], keep4, send4), (tn(d, x[...]) + old3[...], keep3, send3)):
            for i in range(per):
                for y in range(2):
                    lo = total[(i * 4 + y * 2) * blk:(i * 4 + y * 2 + 1) * blk].astype(BF16)
                    hi = total[(i * 4 + y * 2 + 1) * blk:(i * 4 + y * 2 + 2) * blk].astype(BF16)
                    at_ = (i ^ (ids[0] & (per - 1)), y ^ (ids[1] >> 1))

                    @pl.when(core == 0)
                    def _(at_=at_, lo=lo, hi=hi, mine=mine, other=other):
                        mine[at_] = lo
                        other[at_] = hi

                    @pl.when(core == 1)
                    def _(at_=at_, lo=lo, hi=hi, mine=mine, other=other):
                        mine[at_] = hi
                        other[at_] = lo
    else:
        grad4[...] = tn(a, og[0])
        grad3[...] = tn(d, x[...])

    @pl.when(step == last)
    def _():
        load_ct.wait()
        gc[...] = jnp.sum(acc_i[0:R, :], 0, keepdims=True)
        total = jnp.zeros((1, W), F32)
        for p in range(nb // 2):
            pair = []
            for b in (2 * p, 2 * p + 1):
                rows = pl.ds(b * P_, P_)
                lo = (b % 2) * q
                v = jnp.concatenate([bufi[j, p][0:P_, lo:lo + q].astype(F32) for j in range(4)], axis=1)
                out[b] = (v + keep2[half * nb + b] * acc_o[rows, :]).astype(BF16)
                e = acc_i[rows, :]
                n = nrm[b, 0:P_, :]
                total = total + jnp.sum(e * n, 0, keepdims=True)
                e = e * g2[...]
                m1 = jnp.mean(e, 1, keepdims=True)
                m2 = jnp.mean(e * n, 1, keepdims=True)
                pair.append(ct[b].astype(F32) + r2s[b, 0:P_, 0:1] * (e - m1 - n * m2))
            for j in range(4):
                bufo[j, p, 0:P_, :] = jnp.concatenate([v[:, j * q:(j + 1) * q] for v in pair], axis=1).astype(BF16)
                bufo[j, p, P_:, :] = jnp.zeros((PP - P_, 2 * q), BF16)
        gg[...] = total
        for k, o in enumerate((s0, s1, s2, s3)):
            o[...] = bufo[ids[1] ^ k]


def chan_call(ids, keep2, pieces, cot, og, half, w1, w2, b1, b2, g2, c2, before, dp, fb=768):
    images, P_, W = cot.shape
    nb = images // 2
    R = og.shape[1]
    F = w1.shape[1]
    blk = F // (dp * 4)
    per = fb // (4 * blk)
    line = pl.BlockSpec((1, fb), lambda i, ids: (0, i))
    pin = lambda dims: pl.BlockSpec(dims, lambda i, ids: (0,) * len(dims))
    smem = pl.BlockSpec(memory_space=pltpu.SMEM)
    piece = pieces[0].shape
    placed = pl.BlockSpec((per, 2, blk, W), lambda i, ids: (dp_place(i * per ^ ids[0], dp) // per, 0, 0, 0))
    in_specs = [smem] + [pin(piece)] * 4 + [ANY, pl.BlockSpec((1, R, W), lambda i, ids: (half, 0, 0)),
                pl.BlockSpec((W, fb), lambda i, ids: (0, i)), pl.BlockSpec((fb, W), lambda i, ids: (i, 0)),
                line, pin((1, W)), pin((1, W)), pin((1, W))]
    args = [ids, keep2, *pieces, cot, og, w1, w2, b1, b2, g2, c2]
    if half:
        in_specs += [ANY, ANY, ANY]
        args += list(before)
        grads, grad_specs = [shape((dp, 2, blk, W), BF16)] * 4, [placed] * 4
        scratch = [pltpu.VMEM((fb, W), F32), pltpu.VMEM((fb, W), F32), pltpu.SemaphoreType.DMA((2,))]
    else:
        grads, grad_specs = [shape((F, W))] * 2, [pl.BlockSpec((fb, W), lambda i, ids: (i, 0))] * 2
        scratch = []
    n = len(grads)
    return pl.pallas_call(
        functools.partial(chan_kernel, nb=nb, P_=P_, R=R, half=half, dp=dp, blk=blk),
        grid_spec=pltpu.PrefetchScalarGridSpec(
            num_scalar_prefetch=1, grid=(F // fb,), in_specs=in_specs,
            out_specs=grad_specs + [line, pl.BlockSpec((nb, P_, W), lambda i, ids: (half, 0, 0))] + [pin(piece)] * 4
                      + [pin((1, W)), pin((1, W))],
            scratch_shapes=[pltpu.VMEM((R, W), BF16), pltpu.VMEM((nb, piece[1], W), F32), pltpu.VMEM((nb, piece[1], 128), F32),
                            pltpu.VMEM((R, W), F32), pltpu.VMEM((R + 8, W), F32), pltpu.VMEM((4,) + piece, BF16),
                            pltpu.VMEM((4,) + piece, BF16), pltpu.VMEM((nb, P_, W), BF16), pltpu.SemaphoreType.DMA] + scratch),
        out_shape=grads + [shape((1, F)), shape(cot.shape, BF16)] + [shape(piece, BF16)] * 4 + [shape((1, W)), shape((1, W))],
        input_output_aliases={16: n + 1} if half else {},
        compiler_params=pltpu.CompilerParams(vmem_limit_bytes=LIMIT),
        cost_estimate=cost(1),
        name="channel_mlp",
    )(*args)


def as_row(col, size):
    r = lax.broadcasted_iota(jnp.int32, (size, size), 0)
    c = lax.broadcasted_iota(jnp.int32, (size, size), 1)
    return jnp.sum(jnp.where(r == c, jnp.broadcast_to(col, (size, size)), 0.0), 0, keepdims=True)


VEC = 8


def split_rows(dst, at_, v):
    hi = v.astype(BF16).astype(F32)
    dst[pl.ds(at_, VEC), :] = hi
    dst[pl.ds(at_ + VEC, VEC), :] = v - hi


def back_kernel(ids, keep, t0, t1, t2, t3, p0, p1, p2, p3, act, gp, tok, w_in, w_outT, g1, c1, *rest, half, P_, PP):
    if half:
        before, vecs, _, rest = rest[:7], rest[7:14], rest[14], rest[15:]
        u, o0, o1, o2, o3, ps, gw1, gw2, vec, stage, quarters = rest[:11]
        rest = rest[11:]
    else:
        (u, ps, gw1, gw2, ob1, ob2, og, oc), rest = rest[:8], rest[8:]
    mr, right, wide, gcol, mix, buf, gb1, gb2, gg, gc = rest
    _, width, S = tok.shape
    K = w_in.shape[1]
    p = pl.program_id(0)
    first = half * 2 * pl.num_programs(0)

    @pl.when(p == 0)
    def _():
        join_stats((t0, t1, t2, t3), mr, width)
        gcol[0] = jnp.broadcast_to(column(g1[...], width), (width, S))
        gcol[1] = jnp.broadcast_to(column(c1[...], width), (width, S))
        wide[...] = jnp.zeros_like(wide)
        spread_rows(wide, w_outT, P_, PP)
        right[:, 0:K] = wide[...].astype(BF16)
        right[:, K:] = picker(4 * PP, right.shape[1] - K, P_, PP)
        for o in (gb1, gb2, gg, gc):
            o[...] = jnp.zeros_like(o)
        if half:
            gw1[...] = before[0][...]
            gw2[...] = before[1][...]
            ps[...] = before[6][...]
        else:
            for o in (gw1, gw2, ps):
                o[...] = jnp.zeros_like(o)

    for k, o in enumerate((p0, p1, p2, p3)):
        buf[ids[1] ^ k] = o[0]
    sg = buf[...].reshape(4 * PP, 2 * width)
    k0, k1 = keep[first + 2 * p], keep[first + 2 * p + 1]
    lanes = lax.broadcasted_iota(jnp.int32, (1, 2 * width), 1)
    gb2[...] += sg.astype(F32) * jnp.where(lanes < width, k0, k1)
    both = tn(sg, right[...])
    rows = lax.broadcasted_iota(jnp.int32, (2 * width, 1), 0)
    pre1 = ((both[:, 0:K] * gp[...].astype(F32)) * jnp.where(rows < width, k0, k1)).astype(BF16)
    gb1[...] += jnp.sum(pre1.astype(F32).reshape(2 * width // 8, 8, K), 0)
    gw2[...] += nn(sg, act[...])
    ng = nt(pre1, w_in[...])
    for i in range(2):
        b = first + 2 * p + i
        part = slice(i * width, (i + 1) * width)
        m = mr[0, pl.ds(b, 1), :]
        r = mr[1, pl.ds(b, 1), :]
        n = (tok[i].astype(F32) - m) * r
        mix[pl.ds(i * width, width), :] = (n * gcol[0] + gcol[1]).astype(BF16)
        v = ng[part, :]
        gg[...] += v * n
        gc[...] += v
        e = v * gcol[0]
        ps[0, pl.ds(b, 1), :] = jnp.sum(e, 0, keepdims=True)
        ps[1, pl.ds(b, 1), :] = jnp.sum(e * n, 0, keepdims=True)
        u[i] = both[part, K:K + S] + r * e
    gw1[...] += tn(mix[...], pre1)

    @pl.when(p == pl.num_programs(0) - 1)
    def _():
        sums = [jnp.sum(gb1[...], 0, keepdims=True),
                as_row(jnp.sum(gb2[...], 1, keepdims=True), 4 * PP),
                as_row(jnp.sum(gg[...], 1, keepdims=True), width),
                as_row(jnp.sum(gc[...], 1, keepdims=True), width)]
        if not half:
            for v, o in zip(sums, (ob1, ob2, og, oc)):
                o[...] = v
            return
        sums = [v + q[...] for v, q in zip(sums, before[2:6])]
        chan = ids[1]
        vec[...] = jnp.zeros_like(vec)
        row = 0
        for v in (vecs[0][...] + vecs[1][...], vecs[2][...] + vecs[3][...], vecs[4][...] + vecs[5][...], vecs[6][...]):
            for r in range(v.shape[1] // K):
                vec[row:row + 1, :] = v[:, r * K:(r + 1) * K]
                row += 1
        vec[row:row + 1, :] = sums[0]
        vec[row + 1:row + 2, 0:4 * PP] = sums[1]
        row += 2
        mine = jnp.logical_and(lanes >= (chan & 1) * width, lanes < (chan & 1) * width + width)
        for v in sums[2:]:
            twice = jnp.concatenate([v, v], axis=1)
            for r in range(2):
                vec[row:row + 1, :] = jnp.where(jnp.logical_and(mine, (chan >> 1) == r), twice, 0.0)
                row += 1
        stage[...] = jnp.zeros_like(stage)
        for j in range(4):
            stage[0:P_, :] = gw1[j * P_:(j + 1) * P_, :]
            stage[PP:2 * PP, :] = gw2[j * PP:(j + 1) * PP, :]
            split_rows(stage, 2 * PP, vec[j * VEC:(j + 1) * VEC, :])
            for i in range(2):
                stage[pl.ds(2 * PP + 2 * VEC + i * ps.shape[1], ps.shape[1]), 0:S] = ps[i]
            quarters[j] = stage[...].astype(BF16)
        for k, o in enumerate((o0, o1, o2, o3)):
            o[...] = quarters[chan ^ k]


def back_call(ids, keep, stats, pieces, act, gp, tok, w_in, w_outT, g1, c1, half, P_, PP, before, vecs, u_before):
    images, width, S = tok.shape
    nb = images // 2
    K = w_in.shape[1]
    sums = [(S, K), (4 * PP, K), (1, K), (1, 4 * PP), (1, width), (1, width)]
    quarter = (-(-(2 * PP + 2 * VEC + 2 * images) // 16) * 16, K)
    args = [ids, keep, *stats, *pieces, act, gp, tok, w_in, w_outT, g1, c1]
    rows = pl.BlockSpec((2 * width, K), lambda i: (i, 0))
    pairs = pl.BlockSpec((2, width, S), lambda i: (half * (nb // 2) + i, 0, 0))
    in_specs = ([SMEM, SMEM] + [whole(stats[0].shape)] * 4 + [pl.BlockSpec((1, PP, 2 * width), lambda i: (i, 0, 0))] * 4
                + [rows, rows, pairs, whole(w_in.shape), whole(w_outT.shape), whole(g1.shape), whole(c1.shape)])
    outs, out_specs, scratch = [shape((images, width, S))], [pairs], []
    if half:
        args += [*before, *vecs, u_before]
        in_specs += [whole(v.shape) for v in before] + [whole(v.shape) for v in vecs] + [ANY]
        outs += [shape(quarter, BF16)] * 4
        out_specs += [whole(quarter)] * 4
        scratch = [pltpu.VMEM((2, images, S), F32), pltpu.VMEM(sums[0], F32), pltpu.VMEM(sums[1], F32), pltpu.VMEM((4 * VEC, K), F32), pltpu.VMEM(quarter, F32),
                   pltpu.VMEM((4,) + quarter, BF16)]
    else:
        outs += [shape((2, images, S))] + [shape(v) for v in sums]
        out_specs += [whole((2, images, S))] + [whole(v) for v in sums]
    return pl.pallas_call(
        functools.partial(back_kernel, half=half, P_=P_, PP=PP),
        grid=(nb // 2,), in_specs=in_specs, out_specs=out_specs, out_shape=outs,
        scratch_shapes=scratch + [pltpu.VMEM((2, images, S), F32), pltpu.VMEM((4 * PP, K + 256), BF16), pltpu.VMEM((4 * PP, K), F32),
                        pltpu.VMEM((2, width, S), F32), pltpu.VMEM((2 * width, S), BF16), pltpu.VMEM((4, PP, 2 * width), BF16),
                        pltpu.VMEM((8, K), F32), pltpu.VMEM((4 * PP, 2 * width), F32), pltpu.VMEM((width, S), F32),
                        pltpu.VMEM((width, S), F32)],
        input_output_aliases={len(args) - 1: 0} if half else {},
        compiler_params=pltpu.CompilerParams(vmem_limit_bytes=LIMIT * 24 // 60),
        cost_estimate=cost(1),
        name="token_backward",
    )(*args)


def finish_kernel(t0, t1, t2, t3, s0, s1, s2, s3, u, tok, out, mr, sums, *, skip):
    nb, width, S = tok.shape
    first = pl.program_id(0) * nb

    @pl.when(pl.program_id(0) == 0)
    def _():
        join_stats((t0, t1, t2, t3), mr, width)
        total = ((s0[...].astype(F32) + s1[...].astype(F32)) + (s2[...].astype(F32) + s3[...].astype(F32))) * (1.0 / (4 * width))
        images = sums.shape[1]
        for i in range(2):
            sums[i] = total[skip + i * images:skip + (i + 1) * images, 0:S]

    for b in range(nb):
        at_ = pl.ds(first + b, 1)
        r = mr[1, at_, :]
        n = (tok[b].astype(F32) - mr[0, at_, :]) * r
        out[b] = u[b] - r * (sums[0, at_, :] + n * sums[1, at_, :])


def finish_call(stats, sums, u, tok, skip, steps=4):
    images, width, S = tok.shape
    part = pl.BlockSpec((images // steps, width, S), lambda i: (i, 0, 0))
    return pl.pallas_call(
        functools.partial(finish_kernel, skip=skip),
        grid=(steps,),
        in_specs=[whole(stats[0].shape)] * 4 + [whole(sums[0].shape)] * 4 + [part, part],
        out_specs=part,
        out_shape=shape((images, width, S)),
        scratch_shapes=[pltpu.VMEM((2, images, S), F32), pltpu.VMEM((2, images, S), F32)],
        compiler_params=pltpu.CompilerParams(vmem_limit_bytes=LIMIT * 24 // 60),
        cost_estimate=cost(0),
        name="norm_backward",
    )(*stats, *sums, u, tok)


def masks_of(dp):
    return [6, 2, 1] if dp == 8 else [1 << k for k in reversed(range(dp.bit_length() - 1))]


def dp_place(rel, dp):
    return rel ^ ((rel >> 1) & 2) if dp == 8 else rel


UNITS = 6
GROUPS = 3


def orders(dims):
    last, *most = dims
    if len(dims) == 4:
        a, x, y = most
        most = [x, y, a]
    return [(*most[g % len(most):], *most[:g % len(most)], last) for g in range(GROUPS)]


def first_kernel(k4, r4, k3, r3, *outs, plans):
    dp, _, blk, W = k4.shape
    n = 2 * dp
    bits = n.bit_length() - 1
    unit = 2 * W // UNITS
    per = UNITS // GROUPS
    for g, plan in enumerate(plans):
        for i in range(n):
            coord = [(i >> (bits - 1 - d)) & 1 for d in plan]
            j = 0
            for v in coord[1:]:
                j = 2 * j + v
            for m in range(per):
                k, r = (k4, r4) if g * per + m < UNITS // 2 else (k3, r3)
                c = pl.ds((g * per + m) % (UNITS // 2) * unit, unit)
                v = k[i // 2, i % 2, :, c].astype(F32) + r[i // 2, i % 2, :, c].astype(F32)
                outs[g + GROUPS * coord[0]][j, :, m * unit:(m + 1) * unit] = v.astype(BF16)


def next_kernel(*refs):
    ins, outs = refs[:2 * GROUPS], refs[2 * GROUPS:]
    for g in range(GROUPS):
        k, r = ins[2 * g], ins[2 * g + 1]
        n = k.shape[0] // 2
        outs[g][...] = (k[0:n].astype(F32) + r[0:n].astype(F32)).astype(BF16)
        v = (k[n:].astype(F32) + r[n:].astype(F32)).astype(BF16)
        if n > 1:
            outs[GROUPS + g][...] = v
        else:
            outs[GROUPS][g] = v[0]


def last_kernel(*refs):
    ins, got, outs = refs[:GROUPS], refs[GROUPS], refs[GROUPS + 1:]
    unit = 2 * outs[0].shape[1] // UNITS
    per = UNITS // GROUPS
    for g in range(GROUPS):
        v = ins[g][0].astype(F32) + got[g].astype(F32)
        for m in range(per):
            u = g * per + m
            outs[u // (UNITS // 2)][:, u % (UNITS // 2) * unit:(u % (UNITS // 2) + 1) * unit] = v[:, m * unit:(m + 1) * unit]


def plain_call(kernel, args, outs, name, weight=0):
    return pl.pallas_call(
        kernel, grid=(1,), in_specs=[whole(a.shape) for a in args], out_specs=[whole(o.shape) for o in outs], out_shape=outs,
        compiler_params=pltpu.CompilerParams(vmem_limit_bytes=LIMIT * 24 // 60), name=name, cost_estimate=cost(weight))(*args)


def swap(v, mask, world):
    return lax.ppermute(v, ("dp", "chan"), [(i, i ^ mask) for i in range(world)])


def after(values, done):
    *values, _ = lax.optimization_barrier((*values, done))
    return values


def start_sums(keep4, send4, keep3, send3):
    dp, _, blk, W = keep4.shape
    plans = orders(list(range(len(masks_of(dp)) + 1)))
    return plain_call(functools.partial(first_kernel, plans=plans), (keep4, swap(send4, 1, dp * 4), keep3, swap(send3, 1, dp * 4)),
                      [shape((dp, blk, 2 * W // GROUPS), BF16)] * (2 * GROUPS), "sum_first")


def send_step(parts, t, dp):
    masks = [4 * m for m in masks_of(dp)] + [2]
    plans = orders(list(range(len(masks))))
    return [*parts[:GROUPS], *(swap(v, masks[plans[g][t]], dp * 4) for g, v in enumerate(parts[GROUPS:]))]


def sum_step(got):
    n, blk, cols = got[0].shape
    if n == 1:
        return plain_call(last_kernel, got, [shape((blk, GROUPS * cols // 2))] * 2, "sum_last")
    sends = [shape((n // 2, blk, cols), BF16)] * GROUPS if n > 2 else [shape((GROUPS, blk, cols), BF16)]
    got = [v for g in range(GROUPS) for v in (got[g], got[GROUPS + g])]
    return plain_call(next_kernel, got, [shape((n // 2, blk, cols), BF16)] * GROUPS + sends, "sum_next")


def join_terms(s, PP):
    v = s[2 * PP:2 * PP + VEC] + s[2 * PP + VEC:2 * PP + 2 * VEC]
    hi = v.astype(BF16).astype(F32)
    return jnp.concatenate([s[0:2 * PP], hi, v - hi], axis=0).astype(BF16)


def quarter_sum_kernel(*refs, PP):
    *ins, out = refs
    v = [q[...].astype(F32) for q in ins]
    out[...] = join_terms((v[0] + v[1]) + (v[2] + v[3]) if len(v) == 4 else v[0] + v[1], PP)


def quarter_sum(ins, PP):
    dims = (2 * PP + 2 * VEC, ins[0].shape[1])
    return plain_call(functools.partial(quarter_sum_kernel, PP=PP), ins, [shape(dims, BF16)], "quarter_sum")[0]


def unpack_kernel(ids, q0, q1, q2, q3, w1, w2, b3, g2, c2, b4, b1, b2, g1, c1, quarters, vec, *, P_, PP):
    K = w1.shape[1]
    for k, q in enumerate((q0, q1, q2, q3)):
        quarters[ids[1] ^ k] = q[...]
    for j in range(4):
        s = quarters[j].astype(F32)
        w1[j * P_:(j + 1) * P_, :] = s[0:P_]
        w2[j * P_:(j + 1) * P_, :] = s[PP:PP + P_]
        vec[j * VEC:(j + 1) * VEC, :] = s[2 * PP:2 * PP + VEC] + s[2 * PP + VEC:2 * PP + 2 * VEC]
    row = 0
    for o in (b3, g2, c2, b4):
        for r in range(o.shape[0] // K):
            o[r * K:(r + 1) * K] = vec[row]
            row += 1
    b1[...] = vec[row]
    v = vec[row + 1:row + 2, :]
    b2[...] = jnp.concatenate([v[:, j * PP:j * PP + P_] for j in range(4)], axis=1)[0]
    row += 2
    for o in (g1, c1):
        for r in range(2):
            o[r * K:(r + 1) * K] = vec[row]
            row += 1


def unpack_call(ids, quarters, S, F, W, P_, PP):
    dims = quarters[0].shape
    K = dims[1]
    outs = [(S, K), (S, K), (F,), (W,), (W,), (W,), (K,), (S,), (W,), (W,)]
    return pl.pallas_call(
        functools.partial(unpack_kernel, P_=P_, PP=PP), grid=(1,),
        in_specs=[SMEM] + [whole(dims)] * 4, out_specs=[whole(o) for o in outs], out_shape=[shape(o) for o in outs],
        scratch_shapes=[pltpu.VMEM((4,) + dims, BF16), pltpu.VMEM((4 * VEC, K), F32)],
        compiler_params=pltpu.CompilerParams(vmem_limit_bytes=LIMIT * 8 // 60), name="unpack", cost_estimate=cost(0))(ids, *quarters)


def exchange(value):
    return [value] + [lax.ppermute(value, "chan", [(i, i ^ k) for i in range(4)]) for k in (1, 2, 3)]


def trade(pieces):
    return [pieces[0]] + [lax.ppermute(pieces[k], "chan", [(i, i ^ k) for i in range(4)]) for k in (1, 2, 3)]


def shards(tokens, ln1_gain, ln1_bias, mix_in, mix_in_bias, mix_out, mix_out_bias, ln2_gain, ln2_bias,
           chan_in, chan_in_bias, chan_out, chan_out_bias, skip_masks, cotangent):
    images, S, width = tokens.shape
    P_ = cotangent.shape[1]
    W = cotangent.shape[2]
    PP = -(-P_ // 8) * 8
    tok = jnp.swapaxes(tokens, 1, 2)
    w_outT = jnp.swapaxes(mix_out, 0, 1)
    row = lambda v: v.reshape(1, -1)
    chan = lax.axis_index("chan")
    keep1 = skip_masks[:, 0].astype(F32)
    keep2 = skip_masks[:, 1].astype(F32)
    g1, c1 = row(ln1_gain), row(ln1_bias)

    stats = exchange(stats_call(tok))
    halves = (0, 1)
    dp = lax.axis_size("dp")
    ids = jnp.stack([lax.axis_index("dp"), chan]).astype(jnp.int32)
    R = -(-(images // 2) * P_ // 16) * 16
    og, sum_b4 = upstream_call(keep2, cotangent, R)
    fwd = [token_call(ids, keep1, stats, tok, mix_in, row(mix_in_bias), w_outT, row(mix_out_bias), g1, c1, h, P_, PP) for h in halves]
    arrived = [trade(f[2:6]) for f in fwd]
    weights = (chan_in, chan_out, row(chan_in_bias), row(chan_out_bias), row(ln2_gain), row(ln2_bias))
    c0 = chan_call(ids, keep2, arrived[0], cotangent, og, 0, *weights, None, dp)
    part4, part3, b3_0, out = c0[:4]
    c1_ = chan_call(ids, keep2, arrived[1], cotangent, og, 1, *weights, (part4, part3, out), dp)
    keep4, send4, keep3, send3, b3_1, out = c1_[:6]
    tails = (c0[4:], c1_[6:])
    returned = [trade(t[:4]) for t in tails]
    vecs = [b3_0, b3_1, tails[0][4], tails[1][4], tails[0][5], tails[1][5], sum_b4]
    tokens_back = functools.partial(back_call, ids, keep1, stats)
    u, *sums = tokens_back(returned[0], *fwd[0][:2], tok, mix_in, w_outT, g1, c1, 0, P_, PP, None, None, None)
    keep4, keep3 = after((keep4, keep3), u)
    parts = after(start_sums(keep4, send4, keep3, send3), returned[1][3])
    pairs = send_step(parts, 0, dp)
    u, = after((u,), parts[0])
    u, *pieces = tokens_back(returned[1], *fwd[1][:2], tok, mix_in, w_outT, g1, c1, 1, P_, PP, [*sums[1:], sums[0]], vecs, u)
    pieces = trade(pieces)
    quarter = quarter_sum(pieces, PP)
    masks = [4 * m for m in reversed(masks_of(dp))]
    grad = None
    for t, mask in enumerate(masks):
        other = swap(quarter, mask, dp * 4)
        parts = sum_step(after(pairs, quarter))
        pairs = send_step(parts, t + 1, dp)
        done = parts[0]
        if grad is None:
            done = grad = finish_call(stats, after(pieces, done), u, tok, 2 * PP + 2 * VEC)
        quarter = quarter_sum(after((quarter, other), done), PP)
    share_w4, share_w3 = sum_step(after(pairs, quarter))
    s_w1, s_w2, s_b3, s_g2, s_c2, s_b4, s_b1, s_b2, s_g1, s_c1 = unpack_call(
        ids, exchange(quarter), S, chan_in.shape[1], W, P_, PP)
    return (out, jnp.swapaxes(grad, 1, 2), s_g1, s_c1, s_w1, s_b1, jnp.swapaxes(s_w2, 0, 1), s_b2, s_g2, s_c2,
            jnp.swapaxes(share_w3, 0, 1), s_b3, share_w4, s_b4)


def solution(mesh):
    rep = P()
    return jax.shard_map(
        shards, mesh=mesh,
        in_specs=(P("dp", None, "chan"), P("chan"), P("chan")) + (rep,) * 10 + (P("dp", None), P("dp", "chan", None)),
        out_specs=(P("dp", "chan", None), P("dp", None, "chan"), rep, rep, rep, rep, rep, rep, rep, rep,
                   P(None, ("dp", "chan")), rep, P(("dp", "chan"), None), rep),
        check_vma=False,
    )
```

```python
import functools

import jax
import jax.numpy as jnp
from jax import lax
from jax.experimental import pallas as pl
from jax.experimental.pallas import tpu as pltpu
from jax.sharding import PartitionSpec as P

F32, BF16 = jnp.float32, jnp.bfloat16
EPS = 1e-6
RSQRT2 = 0.7071067811865476
RSQRT2PI = 0.3989422804014327
LIMIT = 60 * 2**20
ANY = pl.BlockSpec(memory_space=pl.ANY)
SMEM = pl.BlockSpec(memory_space=pltpu.SMEM)


def nn(a, b):
    return jnp.dot(a, b, preferred_element_type=F32)


def nt(a, b):
    return lax.dot_general(a, b, (((1,), (1,)), ((), ())), preferred_element_type=F32)


def tn(a, b):
    return lax.dot_general(a, b, (((0,), (0,)), ((), ())), preferred_element_type=F32)


def gelu_pair(x):
    half = 0.5 + 0.5 * lax.erf(x * RSQRT2)
    return x * half, half + x * (RSQRT2PI * jnp.exp(-0.5 * (x * x)))


def shape(dims, dtype=F32):
    return jax.ShapeDtypeStruct(dims, dtype)


def cost(weight):
    return pl.CostEstimate(flops=10**11 * weight + 1, bytes_accessed=1, transcendentals=0)


def whole(dims):
    zeros = (0,) * len(dims)
    return pl.BlockSpec(dims, lambda i: zeros)


def at(dims, first):
    rest = (0,) * (len(dims) - 1)
    return pl.BlockSpec(dims, lambda i: (first,) + rest)


def column(row, size):
    r = lax.broadcasted_iota(jnp.int32, (size, size), 0)
    c = lax.broadcasted_iota(jnp.int32, (size, size), 1)
    return jnp.sum(jnp.where(r == c, jnp.broadcast_to(row, (size, size)), 0.0), 1, keepdims=True)


def stats_kernel(tok, out):
    images, width, _ = tok.shape
    first = pl.program_id(0) * images
    for b in range(images):
        x = tok[b].astype(F32)
        m = jnp.sum(x, 0, keepdims=True) * (1.0 / width)
        o = x - m
        out[0, pl.ds(first + b, 1), :] = m
        out[1, pl.ds(first + b, 1), :] = jnp.sum(o * o, 0, keepdims=True)


def stats_call(tok, steps=4):
    images, width, patches = tok.shape
    return pl.pallas_call(
        stats_kernel,
        grid=(steps,),
        in_specs=[pl.BlockSpec((images // steps, width, patches), lambda i: (i, 0, 0))],
        out_specs=whole((2, images, patches)),
        out_shape=shape((2, images, patches)),
        compiler_params=pltpu.CompilerParams(vmem_limit_bytes=LIMIT * 16 // 60),
        cost_estimate=cost(0),
        name="stats",
    )(tok)


def join_stats(stats, mr, width):
    m = 0.25 * ((stats[0][0] + stats[1][0]) + (stats[2][0] + stats[3][0]))
    q = jnp.zeros_like(m)
    for s in stats:
        o = s[0] - m
        q = q + (s[1] + width * (o * o))
    mr[0] = m
    mr[1] = lax.rsqrt(q * (1.0 / (4 * width)) + EPS)


def spread_rows(dst, src, P_, PP):
    for j in range(4):
        dst[pl.ds(j * PP, P_), :] = src[pl.ds(j * P_, P_), :].astype(F32)


def picker(rows, columns, P_, PP):
    r = lax.broadcasted_iota(jnp.int32, (rows, columns), 0)
    c = lax.broadcasted_iota(jnp.int32, (rows, columns), 1)
    pick = jnp.zeros((rows, columns), F32)
    for j in range(4):
        inside = jnp.logical_and(r >= j * PP, r < j * PP + P_)
        pick = jnp.where(jnp.logical_and(inside, c == r - j * (PP - P_)), 1.0, pick)
    return pick.astype(BF16)


def token_kernel(me, keep, t0, t1, t2, t3, tok, w_in, b_in, w_outT, b_out, g1, c1,
                 s0, s1, s2, s3, mr, left, wide, biasb, gcol, mix, rhs, buf, *, first, P_, PP):
    _, width, S = tok.shape
    K = w_in.shape[1]
    p = pl.program_id(0)

    @pl.when(p == 0)
    def _():
        join_stats((t0, t1, t2, t3), mr, width)
        gcol[0] = jnp.broadcast_to(column(g1[...], width), (width, S))
        gcol[1] = jnp.broadcast_to(column(c1[...], width), (width, S))
        wide[...] = jnp.zeros_like(wide)
        spread_rows(wide, w_outT, P_, PP)
        left[:, 0:K] = wide[...].astype(BF16)
        left[:, K:] = picker(4 * PP, left.shape[1] - K, P_, PP)
        biasb[...] = jnp.zeros_like(biasb)
        bcol = jnp.broadcast_to(column(b_out[...], S), (S, biasb.shape[1]))
        for j in range(4):
            biasb[pl.ds(j * PP, P_), :] = bcol[j * P_:(j + 1) * P_, :]
        rhs[...] = jnp.zeros_like(rhs)

    for i in range(2):
        b = first + 2 * p + i
        raw = tok[i]
        m = mr[0, pl.ds(b, 1), :]
        r = mr[1, pl.ds(b, 1), :]
        mix[pl.ds(i * width, width), :] = (((raw.astype(F32) - m) * r) * gcol[0] + gcol[1]).astype(BF16)
        rhs[pl.ds(i * width, width), K:K + S] = raw
    g, _ = gelu_pair(nn(mix[...], w_in[...]) + b_in[...])
    k0, k1 = keep[first + 2 * p], keep[first + 2 * p + 1]
    rows = lax.broadcasted_iota(jnp.int32, (2 * width, 1), 0)
    rhs[:, 0:K] = (g * jnp.where(rows < width, k0, k1)).astype(BF16)
    lanes = lax.broadcasted_iota(jnp.int32, (1, 2 * width), 1)
    out = nt(left[...], rhs[...]) + biasb[...] * jnp.where(lanes < width, k0, k1)
    for j in range(4):
        buf[j] = out[j * PP:(j + 1) * PP, :].astype(BF16)
    for k, o in enumerate((s0, s1, s2, s3)):
        o[0] = buf[me[1] ^ k]


def token_call(ids, keep, stats, tok, w_in, b_in, w_outT, b_out, g1, c1, half, P_, PP):
    images, width, S = tok.shape
    nb = images // 2
    K = w_in.shape[1]
    piece = shape((nb // 2, PP, 2 * width), BF16)
    send = pl.BlockSpec((1, PP, 2 * width), lambda i: (i, 0, 0))
    return pl.pallas_call(
        functools.partial(token_kernel, first=half * nb, P_=P_, PP=PP),
        grid=(nb // 2,),
        in_specs=[SMEM, SMEM] + [whole(stats[0].shape)] * 4
                 + [pl.BlockSpec((2, width, S), lambda i: (half * (nb // 2) + i, 0, 0)), whole(w_in.shape), whole(b_in.shape),
                    whole(w_outT.shape), whole(b_out.shape), whole(g1.shape), whole(c1.shape)],
        out_specs=[send] * 4,
        out_shape=[piece] * 4,
        scratch_shapes=[pltpu.VMEM((2, images, S), F32), pltpu.VMEM((4 * PP, K + 256), BF16), pltpu.VMEM((4 * PP, K), F32),
                        pltpu.VMEM((4 * PP, 2 * width), F32), pltpu.VMEM((2, width, S), F32), pltpu.VMEM((2 * width, S), BF16),
                        pltpu.VMEM((2 * width, K + 256), BF16), pltpu.VMEM((4, PP, 2 * width), BF16)],
        compiler_params=pltpu.CompilerParams(vmem_limit_bytes=LIMIT * 16 // 60),
        cost_estimate=cost(half),
        name="token_forward",
    )(ids, keep, *stats, tok, w_in, b_in, w_outT, b_out, g1, c1)


def upstream_kernel(keep, cot, og, b4, packed, *, P_):
    nb = cot.shape[0]
    rows = nb * P_
    half = pl.program_id(0)

    @pl.when(half == 0)
    def _():
        b4[...] = jnp.zeros_like(b4)
        packed[pl.ds(rows, packed.shape[0] - rows), :] = jnp.zeros((packed.shape[0] - rows, packed.shape[1]), F32)

    for b in range(nb):
        packed[pl.ds(b * P_, P_), :] = cot[b].astype(F32) * keep[half * nb + b]
    v = packed[...]
    og[0] = v.astype(BF16)
    b4[...] += jnp.sum(v, 0, keepdims=True)


def upstream_call(keep, cot, R):
    images, P_, W = cot.shape
    return pl.pallas_call(
        functools.partial(upstream_kernel, P_=P_),
        grid=(2,),
        in_specs=[SMEM, pl.BlockSpec((images // 2, P_, W), lambda i: (i, 0, 0))],
        out_specs=[pl.BlockSpec((1, R, W), lambda i: (i, 0, 0)), whole((1, W))],
        out_shape=[shape((2, R, W), BF16), shape((1, W))],
        scratch_shapes=[pltpu.VMEM((R, W), F32)],
        compiler_params=pltpu.CompilerParams(vmem_limit_bytes=LIMIT * 24 // 60),
        cost_estimate=cost(0),
        name="upstream",
    )(keep, cot)


def chan_kernel(*refs, nb, P_, R, half, dp, blk):
    (ids, keep2, p0, p1, p2, p3, cot, og, w1, w2, b1, b2, g2, c2), refs = refs[:14], refs[14:]
    if half:
        (before4, before3, _, keep4, send4, keep3, send3), refs = refs[:7], refs[7:]
    else:
        (grad4, grad3), refs = refs[:2], refs[2:]
    (b3, out, s0, s1, s2, s3, gg, gc, x, nrm, r2s, acc_o, acc_i, bufi, bufo, ct, ct_sem, ag, act, dact), refs = refs[:20], refs[20:]
    step = pl.program_id(0)
    last = pl.num_programs(0) - 1
    W = x.shape[1]
    fb = w1.shape[1]
    q = W // 4
    PP = bufi.shape[2]
    load_ct = pltpu.make_async_copy(cot.at[pl.ds(half * nb, nb)], ct, ct_sem)
    if half:
        old4, old3, old_sem = refs
        here = pl.ds(step * fb, fb)
        load4 = pltpu.make_async_copy(before4.at[here], old4, old_sem.at[0])
        load3 = pltpu.make_async_copy(before3.at[here], old3, old_sem.at[1])
        load4.start()
        load3.start()

    @pl.when(step == 0)
    def _():
        load_ct.start()
        for k, p in enumerate((p0, p1, p2, p3)):
            bufi[ids[1] ^ k] = p[...]
        for b in range(nb):
            lo = (b % 2) * q
            v = jnp.concatenate([bufi[j, b // 2][:, lo:lo + q].astype(F32) for j in range(4)], axis=1)
            o = v - jnp.mean(v, 1, keepdims=True)
            rr = lax.rsqrt(jnp.mean(o * o, 1, keepdims=True) + EPS)
            n = o * rr
            nrm[b] = n
            r2s[b] = jnp.broadcast_to(rr, (PP, 128))
            acc_i[pl.ds(b * P_, PP), :] = n * g2[...] + c2[...]
        x[...] = acc_i[0:R, :].astype(BF16)
        ag[...] = nt(og[0], w2[...])
        acc_i[...] = jnp.zeros_like(acc_i)
        acc_o[...] = jnp.broadcast_to(b2[...], acc_o.shape)

    @pl.when(step > 0)
    def _():
        ag[...] = nt(og[0], w2[...])

    g, gp = gelu_pair(nn(x[...], w1[...]) + b1[...])
    a = g.astype(BF16)
    d = (ag[...] * gp).astype(BF16)
    b3[...] = jnp.sum(d.astype(F32), 0, keepdims=True)
    acc_o[...] += nn(a, w2[...])
    acc_i[0:R, :] += nt(d, w1[...])
    act[...] = a
    dact[...] = d

    def weight_grads():
        g4 = tn(act[...], og[0])
        g3 = tn(dact[...], x[...])
        if not half:
            grad4[...] = g4
            grad3[...] = g3
            return
        mine_first = (ids[1] & 1) == 0
        per = fb // (4 * blk)
        for total, mine, other in ((g4 + old4[...], keep4, send4), (g3 + old3[...], keep3, send3)):
            for i in range(per):
                for y in range(2):
                    lo = total[(i * 4 + y * 2) * blk:(i * 4 + y * 2 + 1) * blk]
                    hi = total[(i * 4 + y * 2 + 1) * blk:(i * 4 + y * 2 + 2) * blk]
                    at_ = (i ^ (ids[0] & (per - 1)), y ^ (ids[1] >> 1))
                    mine[at_] = jnp.where(mine_first, lo, hi).astype(BF16)
                    other[at_] = jnp.where(mine_first, hi, lo).astype(BF16)

    if half:
        load4.wait()
        load3.wait()

    @pl.when(step < last)
    def _():
        weight_grads()

    @pl.when(step == last)
    def _():
        load_ct.wait()
        weight_grads()
        gc[...] = jnp.sum(acc_i[0:R, :], 0, keepdims=True)
        total = jnp.zeros((1, W), F32)
        for p in range(nb // 2):
            pair = []
            for b in (2 * p, 2 * p + 1):
                rows = pl.ds(b * P_, P_)
                lo = (b % 2) * q
                v = jnp.concatenate([bufi[j, p][0:P_, lo:lo + q].astype(F32) for j in range(4)], axis=1)
                out[b] = (v + keep2[half * nb + b] * acc_o[rows, :]).astype(BF16)
                e = acc_i[rows, :]
                n = nrm[b, 0:P_, :]
                total = total + jnp.sum(e * n, 0, keepdims=True)
                e = e * g2[...]
                m1 = jnp.mean(e, 1, keepdims=True)
                m2 = jnp.mean(e * n, 1, keepdims=True)
                pair.append(ct[b].astype(F32) + r2s[b, 0:P_, 0:1] * (e - m1 - n * m2))
            for j in range(4):
                bufo[j, p, 0:P_, :] = jnp.concatenate([v[:, j * q:(j + 1) * q] for v in pair], axis=1).astype(BF16)
                bufo[j, p, P_:, :] = jnp.zeros((PP - P_, 2 * q), BF16)
        gg[...] = total
        for k, o in enumerate((s0, s1, s2, s3)):
            o[...] = bufo[ids[1] ^ k]


def chan_call(ids, keep2, pieces, cot, og, half, w1, w2, b1, b2, g2, c2, before, dp, fb=768):
    images, P_, W = cot.shape
    nb = images // 2
    R = og.shape[1]
    F = w1.shape[1]
    blk = F // (dp * 4)
    per = fb // (4 * blk)
    line = pl.BlockSpec((1, fb), lambda i, ids: (0, i))
    pin = lambda dims: pl.BlockSpec(dims, lambda i, ids: (0,) * len(dims))
    smem = pl.BlockSpec(memory_space=pltpu.SMEM)
    piece = pieces[0].shape
    placed = pl.BlockSpec((per, 2, blk, W), lambda i, ids: (dp_place(i * per ^ ids[0], dp) // per, 0, 0, 0))
    in_specs = [smem] + [pin(piece)] * 4 + [ANY, pl.BlockSpec((1, R, W), lambda i, ids: (half, 0, 0)),
                pl.BlockSpec((W, fb), lambda i, ids: (0, i)), pl.BlockSpec((fb, W), lambda i, ids: (i, 0)),
                line, pin((1, W)), pin((1, W)), pin((1, W))]
    args = [ids, keep2, *pieces, cot, og, w1, w2, b1, b2, g2, c2]
    if half:
        in_specs += [ANY, ANY, ANY]
        args += list(before)
        grads, grad_specs = [shape((dp, 2, blk, W), BF16)] * 4, [placed] * 4
        scratch = [pltpu.VMEM((fb, W), F32), pltpu.VMEM((fb, W), F32), pltpu.SemaphoreType.DMA((2,))]
    else:
        grads, grad_specs = [shape((F, W))] * 2, [pl.BlockSpec((fb, W), lambda i, ids: (i, 0))] * 2
        scratch = []
    n = len(grads)
    return pl.pallas_call(
        functools.partial(chan_kernel, nb=nb, P_=P_, R=R, half=half, dp=dp, blk=blk),
        grid_spec=pltpu.PrefetchScalarGridSpec(
            num_scalar_prefetch=1, grid=(F // fb,), in_specs=in_specs,
            out_specs=grad_specs + [line, pl.BlockSpec((nb, P_, W), lambda i, ids: (half, 0, 0))] + [pin(piece)] * 4
                      + [pin((1, W)), pin((1, W))],
            scratch_shapes=[pltpu.VMEM((R, W), BF16), pltpu.VMEM((nb, piece[1], W), F32), pltpu.VMEM((nb, piece[1], 128), F32),
                            pltpu.VMEM((R, W), F32), pltpu.VMEM((R + 8, W), F32), pltpu.VMEM((4,) + piece, BF16),
                            pltpu.VMEM((4,) + piece, BF16), pltpu.VMEM((nb, P_, W), BF16), pltpu.SemaphoreType.DMA, pltpu.VMEM((R, fb), F32),
                            pltpu.VMEM((R, fb), BF16), pltpu.VMEM((R, fb), BF16)] + scratch),
        out_shape=grads + [shape((1, F)), shape(cot.shape, BF16)] + [shape(piece, BF16)] * 4 + [shape((1, W)), shape((1, W))],
        input_output_aliases={16: n + 1} if half else {},
        compiler_params=pltpu.CompilerParams(vmem_limit_bytes=LIMIT * 50 // 60),
        cost_estimate=cost(1),
        name="channel_mlp",
    )(*args)


def as_row(col, size):
    r = lax.broadcasted_iota(jnp.int32, (size, size), 0)
    c = lax.broadcasted_iota(jnp.int32, (size, size), 1)
    return jnp.sum(jnp.where(r == c, jnp.broadcast_to(col, (size, size)), 0.0), 0, keepdims=True)


VEC = 8


def split_rows(dst, at_, v):
    hi = v.astype(BF16).astype(F32)
    dst[pl.ds(at_, VEC), :] = hi
    dst[pl.ds(at_ + VEC, VEC), :] = v - hi


def back_kernel(ids, keep, t0, t1, t2, t3, p0, p1, p2, p3, tok, w_in, b_in, w_outT, g1, c1, *rest, half, P_, PP):
    if half:
        before, vecs, _, rest = rest[:7], rest[7:14], rest[14], rest[15:]
        u, o0, o1, o2, o3, ps, gw1, gw2, vec, stage, quarters = rest[:11]
        rest = rest[11:]
    else:
        (u, ps, gw1, gw2, ob1, ob2, og, oc), rest = rest[:8], rest[8:]
    mr, right, wide, gcol, mix, buf, gb1, gb2, gg, gc = rest
    _, width, S = tok.shape
    K = w_in.shape[1]
    p = pl.program_id(0)
    first = half * 2 * pl.num_programs(0)

    @pl.when(p == 0)
    def _():
        join_stats((t0, t1, t2, t3), mr, width)
        gcol[0] = jnp.broadcast_to(column(g1[...], width), (width, S))
        gcol[1] = jnp.broadcast_to(column(c1[...], width), (width, S))
        wide[...] = jnp.zeros_like(wide)
        spread_rows(wide, w_outT, P_, PP)
        right[:, 0:K] = wide[...].astype(BF16)
        right[:, K:] = picker(4 * PP, right.shape[1] - K, P_, PP)
        for o in (gb1, gb2, gg, gc):
            o[...] = jnp.zeros_like(o)
        if half:
            gw1[...] = before[0][...]
            gw2[...] = before[1][...]
            ps[...] = before[6][...]
        else:
            for o in (gw1, gw2, ps):
                o[...] = jnp.zeros_like(o)

    for k, o in enumerate((p0, p1, p2, p3)):
        buf[ids[1] ^ k] = o[0]
    sg = buf[...].reshape(4 * PP, 2 * width)
    k0, k1 = keep[first + 2 * p], keep[first + 2 * p + 1]
    lanes = lax.broadcasted_iota(jnp.int32, (1, 2 * width), 1)
    gb2[...] += sg.astype(F32) * jnp.where(lanes < width, k0, k1)
    both = tn(sg, right[...])
    normed = []
    for i in range(2):
        at_ = pl.ds(first + 2 * p + i, 1)
        n = (tok[i].astype(F32) - mr[0, at_, :]) * mr[1, at_, :]
        mix[pl.ds(i * width, width), :] = (n * gcol[0] + gcol[1]).astype(BF16)
        normed.append(n)
    act, slope = gelu_pair(nn(mix[...], w_in[...]) + b_in[...])
    rows = lax.broadcasted_iota(jnp.int32, (2 * width, 1), 0)
    kept = jnp.where(rows < width, k0, k1)
    pre1 = ((both[:, 0:K] * slope) * kept).astype(BF16)
    gb1[...] += jnp.sum(pre1.astype(F32).reshape(2 * width // 8, 8, K), 0)
    gw2[...] += nn(sg, (act * kept).astype(BF16))
    ng = nt(pre1, w_in[...])
    for i in range(2):
        at_ = pl.ds(first + 2 * p + i, 1)
        part = slice(i * width, (i + 1) * width)
        n, v = normed[i], ng[part, :]
        gg[...] += v * n
        gc[...] += v
        e = v * gcol[0]
        ps[0, at_, :] = jnp.sum(e, 0, keepdims=True)
        ps[1, at_, :] = jnp.sum(e * n, 0, keepdims=True)
        u[i] = both[part, K:K + S] + mr[1, at_, :] * e
    gw1[...] += tn(mix[...], pre1)

    @pl.when(p == pl.num_programs(0) - 1)
    def _():
        sums = [jnp.sum(gb1[...], 0, keepdims=True),
                as_row(jnp.sum(gb2[...], 1, keepdims=True), 4 * PP),
                as_row(jnp.sum(gg[...], 1, keepdims=True), width),
                as_row(jnp.sum(gc[...], 1, keepdims=True), width)]
        if not half:
            for v, o in zip(sums, (ob1, ob2, og, oc)):
                o[...] = v
            return
        sums = [v + q[...] for v, q in zip(sums, before[2:6])]
        chan = ids[1]
        vec[...] = jnp.zeros_like(vec)
        row = 0
        for v in (vecs[0][...] + vecs[1][...], vecs[2][...] + vecs[3][...], vecs[4][...] + vecs[5][...], vecs[6][...]):
            for r in range(v.shape[1] // K):
                vec[row:row + 1, :] = v[:, r * K:(r + 1) * K]
                row += 1
        vec[row:row + 1, :] = sums[0]
        vec[row + 1:row + 2, 0:4 * PP] = sums[1]
        row += 2
        mine = jnp.logical_and(lanes >= (chan & 1) * width, lanes < (chan & 1) * width + width)
        for v in sums[2:]:
            twice = jnp.concatenate([v, v], axis=1)
            for r in range(2):
                vec[row:row + 1, :] = jnp.where(jnp.logical_and(mine, (chan >> 1) == r), twice, 0.0)
                row += 1
        stage[...] = jnp.zeros_like(stage)
        for j in range(4):
            stage[0:P_, :] = gw1[j * P_:(j + 1) * P_, :]
            stage[PP:2 * PP, :] = gw2[j * PP:(j + 1) * PP, :]
            split_rows(stage, 2 * PP, vec[j * VEC:(j + 1) * VEC, :])
            for i in range(2):
                stage[pl.ds(2 * PP + 2 * VEC + i * ps.shape[1], ps.shape[1]), 0:S] = ps[i]
            quarters[j] = stage[...].astype(BF16)
        for k, o in enumerate((o0, o1, o2, o3)):
            o[...] = quarters[chan ^ k]


def back_call(ids, keep, stats, pieces, tok, w_in, b_in, w_outT, g1, c1, half, P_, PP, before, vecs, u_before):
    images, width, S = tok.shape
    nb = images // 2
    K = w_in.shape[1]
    sums = [(S, K), (4 * PP, K), (1, K), (1, 4 * PP), (1, width), (1, width)]
    quarter = (-(-(2 * PP + 2 * VEC + 2 * images) // 16) * 16, K)
    args = [ids, keep, *stats, *pieces, tok, w_in, b_in, w_outT, g1, c1]
    pairs = pl.BlockSpec((2, width, S), lambda i: (half * (nb // 2) + i, 0, 0))
    in_specs = ([SMEM, SMEM] + [whole(stats[0].shape)] * 4 + [pl.BlockSpec((1, PP, 2 * width), lambda i: (i, 0, 0))] * 4
                + [pairs, whole(w_in.shape), whole(b_in.shape), whole(w_outT.shape), whole(g1.shape), whole(c1.shape)])
    outs, out_specs, scratch = [shape((images, width, S))], [pairs], []
    if half:
        args += [*before, *vecs, u_before]
        in_specs += [whole(v.shape) for v in before] + [whole(v.shape) for v in vecs] + [ANY]
        outs += [shape(quarter, BF16)] * 4
        out_specs += [whole(quarter)] * 4
        scratch = [pltpu.VMEM((2, images, S), F32), pltpu.VMEM(sums[0], F32), pltpu.VMEM(sums[1], F32), pltpu.VMEM((4 * VEC, K), F32), pltpu.VMEM(quarter, F32),
                   pltpu.VMEM((4,) + quarter, BF16)]
    else:
        outs += [shape((2, images, S))] + [shape(v) for v in sums]
        out_specs += [whole((2, images, S))] + [whole(v) for v in sums]
    return pl.pallas_call(
        functools.partial(back_kernel, half=half, P_=P_, PP=PP),
        grid=(nb // 2,), in_specs=in_specs, out_specs=out_specs, out_shape=outs,
        scratch_shapes=scratch + [pltpu.VMEM((2, images, S), F32), pltpu.VMEM((4 * PP, K + 256), BF16), pltpu.VMEM((4 * PP, K), F32),
                        pltpu.VMEM((2, width, S), F32), pltpu.VMEM((2 * width, S), BF16), pltpu.VMEM((4, PP, 2 * width), BF16),
                        pltpu.VMEM((8, K), F32), pltpu.VMEM((4 * PP, 2 * width), F32), pltpu.VMEM((width, S), F32),
                        pltpu.VMEM((width, S), F32)],
        input_output_aliases={len(args) - 1: 0} if half else {},
        compiler_params=pltpu.CompilerParams(vmem_limit_bytes=LIMIT * 24 // 60),
        cost_estimate=cost(1),
        name="token_backward",
    )(*args)


def finish_kernel(t0, t1, t2, t3, s0, s1, s2, s3, u, tok, out, mr, sums, *, skip):
    nb, width, S = tok.shape
    first = pl.program_id(0) * nb

    @pl.when(pl.program_id(0) == 0)
    def _():
        join_stats((t0, t1, t2, t3), mr, width)
        total = ((s0[...].astype(F32) + s1[...].astype(F32)) + (s2[...].astype(F32) + s3[...].astype(F32))) * (1.0 / (4 * width))
        images = sums.shape[1]
        for i in range(2):
            sums[i] = total[skip + i * images:skip + (i + 1) * images, 0:S]

    for b in range(nb):
        at_ = pl.ds(first + b, 1)
        r = mr[1, at_, :]
        n = (tok[b].astype(F32) - mr[0, at_, :]) * r
        out[b] = u[b] - r * (sums[0, at_, :] + n * sums[1, at_, :])


def finish_call(stats, sums, u, tok, skip, steps=4):
    images, width, S = tok.shape
    part = pl.BlockSpec((images // steps, width, S), lambda i: (i, 0, 0))
    return pl.pallas_call(
        functools.partial(finish_kernel, skip=skip),
        grid=(steps,),
        in_specs=[whole(stats[0].shape)] * 4 + [whole(sums[0].shape)] * 4 + [part, part],
        out_specs=part,
        out_shape=shape((images, width, S)),
        scratch_shapes=[pltpu.VMEM((2, images, S), F32), pltpu.VMEM((2, images, S), F32)],
        compiler_params=pltpu.CompilerParams(vmem_limit_bytes=LIMIT * 24 // 60),
        cost_estimate=cost(0),
        name="norm_backward",
    )(*stats, *sums, u, tok)


def masks_of(dp):
    return [6, 2, 1] if dp == 8 else [1 << k for k in reversed(range(dp.bit_length() - 1))]


def dp_place(rel, dp):
    return rel ^ ((rel >> 1) & 2) if dp == 8 else rel


UNITS = 6
GROUPS = 3


def orders(dims):
    last, *most = dims
    if len(dims) == 4:
        a, x, y = most
        most = [x, y, a]
    return [(*most[g % len(most):], *most[:g % len(most)], last) for g in range(GROUPS)]


def first_kernel(k4, r4, k3, r3, *outs, plans):
    dp, _, blk, W = k4.shape
    n = 2 * dp
    bits = n.bit_length() - 1
    unit = 2 * W // UNITS
    per = UNITS // GROUPS
    for g, plan in enumerate(plans):
        for i in range(n):
            coord = [(i >> (bits - 1 - d)) & 1 for d in plan]
            j = 0
            for v in coord[1:]:
                j = 2 * j + v
            for m in range(per):
                k, r = (k4, r4) if g * per + m < UNITS // 2 else (k3, r3)
                c = pl.ds((g * per + m) % (UNITS // 2) * unit, unit)
                v = k[i // 2, i % 2, :, c].astype(F32) + r[i // 2, i % 2, :, c].astype(F32)
                outs[g + GROUPS * coord[0]][j, :, m * unit:(m + 1) * unit] = v.astype(BF16)


def next_kernel(*refs):
    ins, outs = refs[:2 * GROUPS], refs[2 * GROUPS:]
    for g in range(GROUPS):
        k, r = ins[2 * g], ins[2 * g + 1]
        n = k.shape[0] // 2
        outs[g][...] = (k[0:n].astype(F32) + r[0:n].astype(F32)).astype(BF16)
        v = (k[n:].astype(F32) + r[n:].astype(F32)).astype(BF16)
        if n > 1:
            outs[GROUPS + g][...] = v
        else:
            outs[GROUPS][g] = v[0]


def last_kernel(*refs):
    ins, got, outs = refs[:GROUPS], refs[GROUPS], refs[GROUPS + 1:]
    unit = 2 * outs[0].shape[1] // UNITS
    per = UNITS // GROUPS
    for g in range(GROUPS):
        v = ins[g][0].astype(F32) + got[g].astype(F32)
        for m in range(per):
            u = g * per + m
            outs[u // (UNITS // 2)][:, u % (UNITS // 2) * unit:(u % (UNITS // 2) + 1) * unit] = v[:, m * unit:(m + 1) * unit]


def plain_call(kernel, args, outs, name, weight=0):
    return pl.pallas_call(
        kernel, grid=(1,), in_specs=[whole(a.shape) for a in args], out_specs=[whole(o.shape) for o in outs], out_shape=outs,
        compiler_params=pltpu.CompilerParams(vmem_limit_bytes=LIMIT * 24 // 60), name=name, cost_estimate=cost(weight))(*args)


def swap(v, mask, world):
    return lax.ppermute(v, ("dp", "chan"), [(i, i ^ mask) for i in range(world)])


def after(values, done):
    *values, _ = lax.optimization_barrier((*values, done))
    return values


def start_sums(keep4, send4, keep3, send3):
    dp, _, blk, W = keep4.shape
    plans = orders(list(range(len(masks_of(dp)) + 1)))
    return plain_call(functools.partial(first_kernel, plans=plans), (keep4, swap(send4, 1, dp * 4), keep3, swap(send3, 1, dp * 4)),
                      [shape((dp, blk, 2 * W // GROUPS), BF16)] * (2 * GROUPS), "sum_first")


def send_step(parts, t, dp):
    masks = [4 * m for m in masks_of(dp)] + [2]
    plans = orders(list(range(len(masks))))
    return [*parts[:GROUPS], *(swap(v, masks[plans[g][t]], dp * 4) for g, v in enumerate(parts[GROUPS:]))]


def sum_step(got):
    n, blk, cols = got[0].shape
    if n == 1:
        return plain_call(last_kernel, got, [shape((blk, GROUPS * cols // 2))] * 2, "sum_last")
    sends = [shape((n // 2, blk, cols), BF16)] * GROUPS if n > 2 else [shape((GROUPS, blk, cols), BF16)]
    got = [v for g in range(GROUPS) for v in (got[g], got[GROUPS + g])]
    return plain_call(next_kernel, got, [shape((n // 2, blk, cols), BF16)] * GROUPS + sends, "sum_next")


def join_terms(s, PP):
    v = s[2 * PP:2 * PP + VEC] + s[2 * PP + VEC:2 * PP + 2 * VEC]
    hi = v.astype(BF16).astype(F32)
    return jnp.concatenate([s[0:2 * PP], hi, v - hi], axis=0).astype(BF16)


def quarter_sum_kernel(*refs, PP):
    *ins, out = refs
    v = [q[...].astype(F32) for q in ins]
    out[...] = join_terms((v[0] + v[1]) + (v[2] + v[3]) if len(v) == 4 else v[0] + v[1], PP)


def quarter_sum(ins, PP):
    dims = (2 * PP + 2 * VEC, ins[0].shape[1])
    return plain_call(functools.partial(quarter_sum_kernel, PP=PP), ins, [shape(dims, BF16)], "quarter_sum")[0]


def unpack_kernel(ids, q0, q1, q2, q3, w1, w2, b3, g2, c2, b4, b1, b2, g1, c1, quarters, vec, *, P_, PP):
    K = w1.shape[1]
    for k, q in enumerate((q0, q1, q2, q3)):
        quarters[ids[1] ^ k] = q[...]
    for j in range(4):
        s = quarters[j].astype(F32)
        w1[j * P_:(j + 1) * P_, :] = s[0:P_]
        w2[j * P_:(j + 1) * P_, :] = s[PP:PP + P_]
        vec[j * VEC:(j + 1) * VEC, :] = s[2 * PP:2 * PP + VEC] + s[2 * PP + VEC:2 * PP + 2 * VEC]
    row = 0
    for o in (b3, g2, c2, b4):
        for r in range(o.shape[0] // K):
            o[r * K:(r + 1) * K] = vec[row]
            row += 1
    b1[...] = vec[row]
    v = vec[row + 1:row + 2, :]
    b2[...] = jnp.concatenate([v[:, j * PP:j * PP + P_] for j in range(4)], axis=1)[0]
    row += 2
    for o in (g1, c1):
        for r in range(2):
            o[r * K:(r + 1) * K] = vec[row]
            row += 1


def unpack_call(ids, quarters, S, F, W, P_, PP):
    dims = quarters[0].shape
    K = dims[1]
    outs = [(S, K), (S, K), (F,), (W,), (W,), (W,), (K,), (S,), (W,), (W,)]
    return pl.pallas_call(
        functools.partial(unpack_kernel, P_=P_, PP=PP), grid=(1,),
        in_specs=[SMEM] + [whole(dims)] * 4, out_specs=[whole(o) for o in outs], out_shape=[shape(o) for o in outs],
        scratch_shapes=[pltpu.VMEM((4,) + dims, BF16), pltpu.VMEM((4 * VEC, K), F32)],
        compiler_params=pltpu.CompilerParams(vmem_limit_bytes=LIMIT * 8 // 60), name="unpack", cost_estimate=cost(0))(ids, *quarters)


def exchange(value):
    return [value] + [lax.ppermute(value, "chan", [(i, i ^ k) for i in range(4)]) for k in (1, 2, 3)]


def trade(pieces):
    return [pieces[0]] + [lax.ppermute(pieces[k], "chan", [(i, i ^ k) for i in range(4)]) for k in (1, 2, 3)]


def shards(tokens, ln1_gain, ln1_bias, mix_in, mix_in_bias, mix_out, mix_out_bias, ln2_gain, ln2_bias,
           chan_in, chan_in_bias, chan_out, chan_out_bias, skip_masks, cotangent):
    images, S, width = tokens.shape
    P_ = cotangent.shape[1]
    W = cotangent.shape[2]
    PP = -(-P_ // 8) * 8
    tok = jnp.swapaxes(tokens, 1, 2)
    w_outT = jnp.swapaxes(mix_out, 0, 1)
    row = lambda v: v.reshape(1, -1)
    chan = lax.axis_index("chan")
    keep1 = skip_masks[:, 0].astype(F32)
    keep2 = skip_masks[:, 1].astype(F32)
    g1, c1 = row(ln1_gain), row(ln1_bias)

    stats = exchange(stats_call(tok))
    halves = (0, 1)
    dp = lax.axis_size("dp")
    ids = jnp.stack([lax.axis_index("dp"), chan]).astype(jnp.int32)
    R = -(-(images // 2) * P_ // 16) * 16
    og, sum_b4 = upstream_call(keep2, cotangent, R)
    fwd = [token_call(ids, keep1, stats, tok, mix_in, row(mix_in_bias), w_outT, row(mix_out_bias), g1, c1, h, P_, PP) for h in halves]
    arrived = [trade(f) for f in fwd]
    weights = (chan_in, chan_out, row(chan_in_bias), row(chan_out_bias), row(ln2_gain), row(ln2_bias))
    c0 = chan_call(ids, keep2, arrived[0], cotangent, og, 0, *weights, None, dp)
    part4, part3, b3_0, out = c0[:4]
    c1_ = chan_call(ids, keep2, arrived[1], cotangent, og, 1, *weights, (part4, part3, out), dp)
    keep4, send4, keep3, send3, b3_1, out = c1_[:6]
    tails = (c0[4:], c1_[6:])
    returned = [trade(t[:4]) for t in tails]
    vecs = [b3_0, b3_1, tails[0][4], tails[1][4], tails[0][5], tails[1][5], sum_b4]
    tokens_back = functools.partial(back_call, ids, keep1, stats)
    u, *sums = tokens_back(returned[0], tok, mix_in, row(mix_in_bias), w_outT, g1, c1, 0, P_, PP, None, None, None)
    keep4, keep3 = after((keep4, keep3), u)
    parts = list(start_sums(keep4, send4, keep3, send3))
    parts[GROUPS + 1], = after((parts[GROUPS + 1],), returned[1][3])
    pairs = send_step(parts, 0, dp)
    u, = after((u,), parts[0])
    u, *pieces = tokens_back(returned[1], tok, mix_in, row(mix_in_bias), w_outT, g1, c1, 1, P_, PP, [*sums[1:], sums[0]], vecs, u)
    pieces = trade(pieces)
    quarter = quarter_sum(pieces, PP)
    masks = [4 * m for m in reversed(masks_of(dp))]
    grad = None
    for t, mask in enumerate(masks):
        other = swap(quarter, mask, dp * 4)
        parts = sum_step(after(pairs, quarter))
        pairs = send_step(parts, t + 1, dp)
        done = parts[0]
        if grad is None:
            done = grad = finish_call(stats, after(pieces, done), u, tok, 2 * PP + 2 * VEC)
        quarter = quarter_sum(after((quarter, other), done), PP)
    share_w4, share_w3 = sum_step(after(pairs, quarter))
    s_w1, s_w2, s_b3, s_g2, s_c2, s_b4, s_b1, s_b2, s_g1, s_c1 = unpack_call(
        ids, exchange(quarter), S, chan_in.shape[1], W, P_, PP)
    return (out, jnp.swapaxes(grad, 1, 2), s_g1, s_c1, s_w1, s_b1, jnp.swapaxes(s_w2, 0, 1), s_b2, s_g2, s_c2,
            jnp.swapaxes(share_w3, 0, 1), s_b3, share_w4, s_b4)


def solution(mesh):
    rep = P()
    return jax.shard_map(
        shards, mesh=mesh,
        in_specs=(P("dp", None, "chan"), P("chan"), P("chan")) + (rep,) * 10 + (P("dp", None), P("dp", "chan", None)),
        out_specs=(P("dp", "chan", None), P("dp", None, "chan"), rep, rep, rep, rep, rep, rep, rep, rep,
                   P(None, ("dp", "chan")), rep, P(("dp", "chan"), None), rep),
        check_vma=False,
    )
```

```python
import functools

import jax
import jax.numpy as jnp
from jax import lax
from jax.experimental import pallas as pl
from jax.experimental.pallas import tpu as pltpu
from jax.sharding import PartitionSpec as P

F32, BF16 = jnp.float32, jnp.bfloat16
EPS = 1e-6
RSQRT2 = 0.7071067811865476
RSQRT2PI = 0.3989422804014327
LIMIT = 60 * 2**20
ANY = pl.BlockSpec(memory_space=pl.ANY)
SMEM = pl.BlockSpec(memory_space=pltpu.SMEM)


def nn(a, b):
    return jnp.dot(a, b, preferred_element_type=F32)


def nt(a, b):
    return lax.dot_general(a, b, (((1,), (1,)), ((), ())), preferred_element_type=F32)


def tn(a, b):
    return lax.dot_general(a, b, (((0,), (0,)), ((), ())), preferred_element_type=F32)


def gelu_pair(x):
    half = 0.5 + 0.5 * lax.erf(x * RSQRT2)
    return x * half, half + x * (RSQRT2PI * jnp.exp(-0.5 * (x * x)))


def shape(dims, dtype=F32):
    return jax.ShapeDtypeStruct(dims, dtype)


def cost(weight):
    return pl.CostEstimate(flops=10**11 * weight + 1, bytes_accessed=1, transcendentals=0)


def whole(dims):
    zeros = (0,) * len(dims)
    return pl.BlockSpec(dims, lambda i: zeros)


def at(dims, first):
    rest = (0,) * (len(dims) - 1)
    return pl.BlockSpec(dims, lambda i: (first,) + rest)


def column(row, size):
    r = lax.broadcasted_iota(jnp.int32, (size, size), 0)
    c = lax.broadcasted_iota(jnp.int32, (size, size), 1)
    return jnp.sum(jnp.where(r == c, jnp.broadcast_to(row, (size, size)), 0.0), 1, keepdims=True)


def stats_kernel(tok, out):
    images, width, _ = tok.shape
    first = pl.program_id(0) * images
    for b in range(images):
        x = tok[b].astype(F32)
        m = jnp.sum(x, 0, keepdims=True) * (1.0 / width)
        o = x - m
        out[0, pl.ds(first + b, 1), :] = m
        out[1, pl.ds(first + b, 1), :] = jnp.sum(o * o, 0, keepdims=True)


def stats_call(tok, steps=4):
    images, width, patches = tok.shape
    return pl.pallas_call(
        stats_kernel,
        grid=(steps,),
        in_specs=[pl.BlockSpec((images // steps, width, patches), lambda i: (i, 0, 0))],
        out_specs=whole((2, images, patches)),
        out_shape=shape((2, images, patches)),
        compiler_params=pltpu.CompilerParams(vmem_limit_bytes=LIMIT * 16 // 60),
        cost_estimate=cost(0),
        name="stats",
    )(tok)


def join_stats(stats, mr, width):
    m = 0.25 * ((stats[0][0] + stats[1][0]) + (stats[2][0] + stats[3][0]))
    q = jnp.zeros_like(m)
    for s in stats:
        o = s[0] - m
        q = q + (s[1] + width * (o * o))
    mr[0] = m
    mr[1] = lax.rsqrt(q * (1.0 / (4 * width)) + EPS)


def spread_rows(dst, src, P_, PP):
    for j in range(4):
        dst[pl.ds(j * PP, P_), :] = src[pl.ds(j * P_, P_), :].astype(F32)


def picker(rows, columns, P_, PP):
    r = lax.broadcasted_iota(jnp.int32, (rows, columns), 0)
    c = lax.broadcasted_iota(jnp.int32, (rows, columns), 1)
    pick = jnp.zeros((rows, columns), F32)
    for j in range(4):
        inside = jnp.logical_and(r >= j * PP, r < j * PP + P_)
        pick = jnp.where(jnp.logical_and(inside, c == r - j * (PP - P_)), 1.0, pick)
    return pick.astype(BF16)


def token_kernel(me, keep, t0, t1, t2, t3, tok, w_in, b_in, w_outT, b_out, g1, c1,
                 s0, s1, s2, s3, mr, left, wide, biasb, gcol, mix, rhs, buf, *, first, P_, PP):
    _, width, S = tok.shape
    K = w_in.shape[1]
    p = pl.program_id(0)

    @pl.when(p == 0)
    def _():
        join_stats((t0, t1, t2, t3), mr, width)
        gcol[0] = jnp.broadcast_to(column(g1[...], width), (width, S))
        gcol[1] = jnp.broadcast_to(column(c1[...], width), (width, S))
        wide[...] = jnp.zeros_like(wide)
        spread_rows(wide, w_outT, P_, PP)
        left[:, 0:K] = wide[...].astype(BF16)
        left[:, K:] = picker(4 * PP, left.shape[1] - K, P_, PP)
        biasb[...] = jnp.zeros_like(biasb)
        bcol = jnp.broadcast_to(column(b_out[...], S), (S, biasb.shape[1]))
        for j in range(4):
            biasb[pl.ds(j * PP, P_), :] = bcol[j * P_:(j + 1) * P_, :]
        rhs[...] = jnp.zeros_like(rhs)

    for i in range(2):
        b = first + 2 * p + i
        raw = tok[i]
        m = mr[0, pl.ds(b, 1), :]
        r = mr[1, pl.ds(b, 1), :]
        mix[pl.ds(i * width, width), :] = (((raw.astype(F32) - m) * r) * gcol[0] + gcol[1]).astype(BF16)
        rhs[pl.ds(i * width, width), K:K + S] = raw
    g, _ = gelu_pair(nn(mix[...], w_in[...]) + b_in[...])
    k0, k1 = keep[first + 2 * p], keep[first + 2 * p + 1]
    rows = lax.broadcasted_iota(jnp.int32, (2 * width, 1), 0)
    rhs[:, 0:K] = (g * jnp.where(rows < width, k0, k1)).astype(BF16)
    lanes = lax.broadcasted_iota(jnp.int32, (1, 2 * width), 1)
    out = nt(left[...], rhs[...]) + biasb[...] * jnp.where(lanes < width, k0, k1)
    for j in range(4):
        buf[j] = out[j * PP:(j + 1) * PP, :].astype(BF16)
    for k, o in enumerate((s0, s1, s2, s3)):
        o[0] = buf[me[1] ^ k]


def token_call(ids, keep, stats, tok, w_in, b_in, w_outT, b_out, g1, c1, half, P_, PP):
    images, width, S = tok.shape
    nb = images // 2
    K = w_in.shape[1]
    piece = shape((nb // 2, PP, 2 * width), BF16)
    send = pl.BlockSpec((1, PP, 2 * width), lambda i: (i, 0, 0))
    return pl.pallas_call(
        functools.partial(token_kernel, first=half * nb, P_=P_, PP=PP),
        grid=(nb // 2,),
        in_specs=[SMEM, SMEM] + [whole(stats[0].shape)] * 4
                 + [pl.BlockSpec((2, width, S), lambda i: (half * (nb // 2) + i, 0, 0)), whole(w_in.shape), whole(b_in.shape),
                    whole(w_outT.shape), whole(b_out.shape), whole(g1.shape), whole(c1.shape)],
        out_specs=[send] * 4,
        out_shape=[piece] * 4,
        scratch_shapes=[pltpu.VMEM((2, images, S), F32), pltpu.VMEM((4 * PP, K + 256), BF16), pltpu.VMEM((4 * PP, K), F32),
                        pltpu.VMEM((4 * PP, 2 * width), F32), pltpu.VMEM((2, width, S), F32), pltpu.VMEM((2 * width, S), BF16),
                        pltpu.VMEM((2 * width, K + 256), BF16), pltpu.VMEM((4, PP, 2 * width), BF16)],
        compiler_params=pltpu.CompilerParams(vmem_limit_bytes=LIMIT * 16 // 60),
        cost_estimate=cost(half),
        name="token_forward",
    )(ids, keep, *stats, tok, w_in, b_in, w_outT, b_out, g1, c1)


def upstream_kernel(keep, cot, og, b4, packed, *, P_):
    nb = cot.shape[0]
    rows = nb * P_
    half = pl.program_id(0)

    @pl.when(half == 0)
    def _():
        b4[...] = jnp.zeros_like(b4)
        packed[pl.ds(rows, packed.shape[0] - rows), :] = jnp.zeros((packed.shape[0] - rows, packed.shape[1]), F32)

    for b in range(nb):
        packed[pl.ds(b * P_, P_), :] = cot[b].astype(F32) * keep[half * nb + b]
    v = packed[...]
    og[0] = v.astype(BF16)
    b4[...] += jnp.sum(v, 0, keepdims=True)


def upstream_call(keep, cot, R):
    images, P_, W = cot.shape
    return pl.pallas_call(
        functools.partial(upstream_kernel, P_=P_),
        grid=(2,),
        in_specs=[SMEM, pl.BlockSpec((images // 2, P_, W), lambda i: (i, 0, 0))],
        out_specs=[pl.BlockSpec((1, R, W), lambda i: (i, 0, 0)), whole((1, W))],
        out_shape=[shape((2, R, W), BF16), shape((1, W))],
        scratch_shapes=[pltpu.VMEM((R, W), F32)],
        compiler_params=pltpu.CompilerParams(vmem_limit_bytes=LIMIT * 24 // 60),
        cost_estimate=cost(0),
        name="upstream",
    )(keep, cot)


def chan_kernel(*refs, nb, P_, R, half, dp, blk):
    (ids, keep2, p0, p1, p2, p3, cot, og, w1, w2, b1, b2, g2, c2), refs = refs[:14], refs[14:]
    if half:
        (before4, before3, _, keep4, send4, keep3, send3), refs = refs[:7], refs[7:]
    else:
        (grad4, grad3), refs = refs[:2], refs[2:]
    (b3, out, s0, s1, s2, s3, gg, gc, x, nrm, r2s, acc_o, acc_i, bufi, bufo, ct, ct_sem, ag, act, dact), refs = refs[:20], refs[20:]
    step = pl.program_id(0)
    last = pl.num_programs(0) - 1
    W = x.shape[1]
    fb = w1.shape[1]
    q = W // 4
    PP = bufi.shape[2]
    load_ct = pltpu.make_async_copy(cot.at[pl.ds(half * nb, nb)], ct, ct_sem)
    if half:
        old4, old3, old_sem = refs
        here = pl.ds(step * fb, fb)
        load4 = pltpu.make_async_copy(before4.at[here], old4, old_sem.at[0])
        load3 = pltpu.make_async_copy(before3.at[here], old3, old_sem.at[1])
        load4.start()
        load3.start()

    @pl.when(step == 0)
    def _():
        load_ct.start()
        for k, p in enumerate((p0, p1, p2, p3)):
            bufi[ids[1] ^ k] = p[...]
        for b in range(nb):
            lo = (b % 2) * q
            v = jnp.concatenate([bufi[j, b // 2][:, lo:lo + q].astype(F32) for j in range(4)], axis=1)
            o = v - jnp.mean(v, 1, keepdims=True)
            rr = lax.rsqrt(jnp.mean(o * o, 1, keepdims=True) + EPS)
            n = o * rr
            nrm[b] = n
            r2s[b] = jnp.broadcast_to(rr, (PP, 128))
            acc_i[pl.ds(b * P_, PP), :] = n * g2[...] + c2[...]
        x[...] = acc_i[0:R, :].astype(BF16)
        ag[...] = nt(og[0], w2[...])
        acc_i[...] = jnp.zeros_like(acc_i)
        acc_o[...] = jnp.broadcast_to(b2[...], acc_o.shape)

    @pl.when(step > 0)
    def _():
        ag[...] = nt(og[0], w2[...])

    g, gp = gelu_pair(nn(x[...], w1[...]) + b1[...])
    a = g.astype(BF16)
    d = (ag[...] * gp).astype(BF16)
    b3[...] = jnp.sum(d.astype(F32), 0, keepdims=True)
    acc_o[...] += nn(a, w2[...])
    acc_i[0:R, :] += nt(d, w1[...])
    act[...] = a
    dact[...] = d

    def weight_grads():
        g4 = tn(act[...], og[0])
        g3 = tn(dact[...], x[...])
        if not half:
            grad4[...] = g4
            grad3[...] = g3
            return
        mine_first = (ids[1] & 1) == 0
        per = fb // (4 * blk)
        for total, mine, other in ((g4 + old4[...], keep4, send4), (g3 + old3[...], keep3, send3)):
            for i in range(per):
                for y in range(2):
                    lo = total[(i * 4 + y * 2) * blk:(i * 4 + y * 2 + 1) * blk]
                    hi = total[(i * 4 + y * 2 + 1) * blk:(i * 4 + y * 2 + 2) * blk]
                    at_ = (i ^ (ids[0] & (per - 1)), y ^ (ids[1] >> 1))
                    mine[at_] = jnp.where(mine_first, lo, hi).astype(BF16)
                    other[at_] = jnp.where(mine_first, hi, lo).astype(BF16)

    if half:
        load4.wait()
        load3.wait()

    @pl.when(step < last)
    def _():
        weight_grads()

    @pl.when(step == last)
    def _():
        load_ct.wait()
        weight_grads()
        gc[...] = jnp.sum(acc_i[0:R, :], 0, keepdims=True)
        total = jnp.zeros((1, W), F32)
        for p in range(nb // 2):
            pair = []
            for b in (2 * p, 2 * p + 1):
                rows = pl.ds(b * P_, P_)
                lo = (b % 2) * q
                v = jnp.concatenate([bufi[j, p][0:P_, lo:lo + q].astype(F32) for j in range(4)], axis=1)
                out[b] = (v + keep2[half * nb + b] * acc_o[rows, :]).astype(BF16)
                e = acc_i[rows, :]
                n = nrm[b, 0:P_, :]
                total = total + jnp.sum(e * n, 0, keepdims=True)
                e = e * g2[...]
                m1 = jnp.mean(e, 1, keepdims=True)
                m2 = jnp.mean(e * n, 1, keepdims=True)
                pair.append(ct[b].astype(F32) + r2s[b, 0:P_, 0:1] * (e - m1 - n * m2))
            for j in range(4):
                bufo[j, p, 0:P_, :] = jnp.concatenate([v[:, j * q:(j + 1) * q] for v in pair], axis=1).astype(BF16)
                bufo[j, p, P_:, :] = jnp.zeros((PP - P_, 2 * q), BF16)
        gg[...] = total
        for k, o in enumerate((s0, s1, s2, s3)):
            o[...] = bufo[ids[1] ^ k]


def chan_call(ids, keep2, pieces, cot, og, half, w1, w2, b1, b2, g2, c2, before, dp, fb=768):
    images, P_, W = cot.shape
    nb = images // 2
    R = og.shape[1]
    F = w1.shape[1]
    blk = F // (dp * 4)
    per = fb // (4 * blk)
    line = pl.BlockSpec((1, fb), lambda i, ids: (0, i))
    pin = lambda dims: pl.BlockSpec(dims, lambda i, ids: (0,) * len(dims))
    smem = pl.BlockSpec(memory_space=pltpu.SMEM)
    piece = pieces[0].shape
    placed = pl.BlockSpec((per, 2, blk, W), lambda i, ids: (dp_place(i * per ^ ids[0], dp) // per, 0, 0, 0))
    in_specs = [smem] + [pin(piece)] * 4 + [ANY, pl.BlockSpec((1, R, W), lambda i, ids: (half, 0, 0)),
                pl.BlockSpec((W, fb), lambda i, ids: (0, i)), pl.BlockSpec((fb, W), lambda i, ids: (i, 0)),
                line, pin((1, W)), pin((1, W)), pin((1, W))]
    args = [ids, keep2, *pieces, cot, og, w1, w2, b1, b2, g2, c2]
    if half:
        in_specs += [ANY, ANY, ANY]
        args += list(before)
        grads, grad_specs = [shape((dp, 2, blk, W), BF16)] * 4, [placed] * 4
        scratch = [pltpu.VMEM((fb, W), F32), pltpu.VMEM((fb, W), F32), pltpu.SemaphoreType.DMA((2,))]
    else:
        grads, grad_specs = [shape((F, W))] * 2, [pl.BlockSpec((fb, W), lambda i, ids: (i, 0))] * 2
        scratch = []
    n = len(grads)
    return pl.pallas_call(
        functools.partial(chan_kernel, nb=nb, P_=P_, R=R, half=half, dp=dp, blk=blk),
        grid_spec=pltpu.PrefetchScalarGridSpec(
            num_scalar_prefetch=1, grid=(F // fb,), in_specs=in_specs,
            out_specs=grad_specs + [line, pl.BlockSpec((nb, P_, W), lambda i, ids: (half, 0, 0))] + [pin(piece)] * 4
                      + [pin((1, W)), pin((1, W))],
            scratch_shapes=[pltpu.VMEM((R, W), BF16), pltpu.VMEM((nb, piece[1], W), F32), pltpu.VMEM((nb, piece[1], 128), F32),
                            pltpu.VMEM((R, W), F32), pltpu.VMEM((R + 8, W), F32), pltpu.VMEM((4,) + piece, BF16),
                            pltpu.VMEM((4,) + piece, BF16), pltpu.VMEM((nb, P_, W), BF16), pltpu.SemaphoreType.DMA, pltpu.VMEM((R, fb), F32),
                            pltpu.VMEM((R, fb), BF16), pltpu.VMEM((R, fb), BF16)] + scratch),
        out_shape=grads + [shape((1, F)), shape(cot.shape, BF16)] + [shape(piece, BF16)] * 4 + [shape((1, W)), shape((1, W))],
        input_output_aliases={16: n + 1} if half else {},
        compiler_params=pltpu.CompilerParams(vmem_limit_bytes=LIMIT * 50 // 60),
        cost_estimate=cost(1),
        name="channel_mlp",
    )(*args)


def as_row(col, size):
    r = lax.broadcasted_iota(jnp.int32, (size, size), 0)
    c = lax.broadcasted_iota(jnp.int32, (size, size), 1)
    return jnp.sum(jnp.where(r == c, jnp.broadcast_to(col, (size, size)), 0.0), 0, keepdims=True)


VEC = 8


def split_rows(dst, at_, v):
    hi = v.astype(BF16).astype(F32)
    dst[pl.ds(at_, VEC), :] = hi
    dst[pl.ds(at_ + VEC, VEC), :] = v - hi


def back_kernel(ids, keep, t0, t1, t2, t3, p0, p1, p2, p3, tok, w_in, b_in, w_outT, g1, c1, *rest, half, P_, PP):
    if half:
        before, vecs, _, rest = rest[:7], rest[7:14], rest[14], rest[15:]
        u, o0, o1, o2, o3, ps, gw1, gw2, vec, stage, quarters = rest[:11]
        rest = rest[11:]
    else:
        (u, ps, gw1, gw2, ob1, ob2, og, oc), rest = rest[:8], rest[8:]
    mr, right, wide, gcol, mix, buf, gb1, gb2, gg, gc = rest
    _, width, S = tok.shape
    K = w_in.shape[1]
    p = pl.program_id(0)
    first = half * 2 * pl.num_programs(0)

    @pl.when(p == 0)
    def _():
        join_stats((t0, t1, t2, t3), mr, width)
        gcol[0] = jnp.broadcast_to(column(g1[...], width), (width, S))
        gcol[1] = jnp.broadcast_to(column(c1[...], width), (width, S))
        wide[...] = jnp.zeros_like(wide)
        spread_rows(wide, w_outT, P_, PP)
        right[:, 0:K] = wide[...].astype(BF16)
        right[:, K:] = picker(4 * PP, right.shape[1] - K, P_, PP)
        for o in (gb1, gb2, gg, gc):
            o[...] = jnp.zeros_like(o)
        if half:
            gw1[...] = before[0][...]
            gw2[...] = before[1][...]
            ps[...] = before[6][...]
        else:
            for o in (gw1, gw2, ps):
                o[...] = jnp.zeros_like(o)

    for k, o in enumerate((p0, p1, p2, p3)):
        buf[ids[1] ^ k] = o[0]
    sg = buf[...].reshape(4 * PP, 2 * width)
    k0, k1 = keep[first + 2 * p], keep[first + 2 * p + 1]
    lanes = lax.broadcasted_iota(jnp.int32, (1, 2 * width), 1)
    gb2[...] += sg.astype(F32) * jnp.where(lanes < width, k0, k1)
    both = tn(sg, right[...])
    normed = []
    for i in range(2):
        at_ = pl.ds(first + 2 * p + i, 1)
        n = (tok[i].astype(F32) - mr[0, at_, :]) * mr[1, at_, :]
        mix[pl.ds(i * width, width), :] = (n * gcol[0] + gcol[1]).astype(BF16)
        normed.append(n)
    act, slope = gelu_pair(nn(mix[...], w_in[...]) + b_in[...])
    rows = lax.broadcasted_iota(jnp.int32, (2 * width, 1), 0)
    kept = jnp.where(rows < width, k0, k1)
    pre1 = ((both[:, 0:K] * slope) * kept).astype(BF16)
    gb1[...] += jnp.sum(pre1.astype(F32).reshape(2 * width // 8, 8, K), 0)
    gw2[...] += nn(sg, (act * kept).astype(BF16))
    ng = nt(pre1, w_in[...])
    for i in range(2):
        at_ = pl.ds(first + 2 * p + i, 1)
        part = slice(i * width, (i + 1) * width)
        n, v = normed[i], ng[part, :]
        gg[...] += v * n
        gc[...] += v
        e = v * gcol[0]
        ps[0, at_, :] = jnp.sum(e, 0, keepdims=True)
        ps[1, at_, :] = jnp.sum(e * n, 0, keepdims=True)
        u[i] = both[part, K:K + S] + mr[1, at_, :] * e
    gw1[...] += tn(mix[...], pre1)

    @pl.when(p == pl.num_programs(0) - 1)
    def _():
        sums = [jnp.sum(gb1[...], 0, keepdims=True),
                as_row(jnp.sum(gb2[...], 1, keepdims=True), 4 * PP),
                as_row(jnp.sum(gg[...], 1, keepdims=True), width),
                as_row(jnp.sum(gc[...], 1, keepdims=True), width)]
        if not half:
            for v, o in zip(sums, (ob1, ob2, og, oc)):
                o[...] = v
            return
        sums = [v + q[...] for v, q in zip(sums, before[2:6])]
        chan = ids[1]
        vec[...] = jnp.zeros_like(vec)
        row = 0
        for v in (vecs[0][...] + vecs[1][...], vecs[2][...] + vecs[3][...], vecs[4][...] + vecs[5][...], vecs[6][...]):
            for r in range(v.shape[1] // K):
                vec[row:row + 1, :] = v[:, r * K:(r + 1) * K]
                row += 1
        vec[row:row + 1, :] = sums[0]
        vec[row + 1:row + 2, 0:4 * PP] = sums[1]
        row += 2
        mine = jnp.logical_and(lanes >= (chan & 1) * width, lanes < (chan & 1) * width + width)
        for v in sums[2:]:
            twice = jnp.concatenate([v, v], axis=1)
            for r in range(2):
                vec[row:row + 1, :] = jnp.where(jnp.logical_and(mine, (chan >> 1) == r), twice, 0.0)
                row += 1
        stage[...] = jnp.zeros_like(stage)
        for j in range(4):
            stage[0:P_, :] = gw1[j * P_:(j + 1) * P_, :]
            stage[PP:2 * PP, :] = gw2[j * PP:(j + 1) * PP, :]
            split_rows(stage, 2 * PP, vec[j * VEC:(j + 1) * VEC, :])
            for i in range(2):
                stage[pl.ds(2 * PP + 2 * VEC + i * ps.shape[1], ps.shape[1]), 0:S] = ps[i]
            quarters[j] = stage[...].astype(BF16)
        for k, o in enumerate((o0, o1, o2, o3)):
            o[...] = quarters[chan ^ k]


def back_call(ids, keep, stats, pieces, tok, w_in, b_in, w_outT, g1, c1, half, P_, PP, before, vecs, u_before):
    images, width, S = tok.shape
    nb = images // 2
    K = w_in.shape[1]
    sums = [(S, K), (4 * PP, K), (1, K), (1, 4 * PP), (1, width), (1, width)]
    quarter = (-(-(2 * PP + 2 * VEC + 2 * images) // 16) * 16, K)
    args = [ids, keep, *stats, *pieces, tok, w_in, b_in, w_outT, g1, c1]
    pairs = pl.BlockSpec((2, width, S), lambda i: (half * (nb // 2) + i, 0, 0))
    in_specs = ([SMEM, SMEM] + [whole(stats[0].shape)] * 4 + [pl.BlockSpec((1, PP, 2 * width), lambda i: (i, 0, 0))] * 4
                + [pairs, whole(w_in.shape), whole(b_in.shape), whole(w_outT.shape), whole(g1.shape), whole(c1.shape)])
    outs, out_specs, scratch = [shape((images, width, S))], [pairs], []
    if half:
        args += [*before, *vecs, u_before]
        in_specs += [whole(v.shape) for v in before] + [whole(v.shape) for v in vecs] + [ANY]
        outs += [shape(quarter, BF16)] * 4
        out_specs += [whole(quarter)] * 4
        scratch = [pltpu.VMEM((2, images, S), F32), pltpu.VMEM(sums[0], F32), pltpu.VMEM(sums[1], F32), pltpu.VMEM((4 * VEC, K), F32), pltpu.VMEM(quarter, F32),
                   pltpu.VMEM((4,) + quarter, BF16)]
    else:
        outs += [shape((2, images, S))] + [shape(v) for v in sums]
        out_specs += [whole((2, images, S))] + [whole(v) for v in sums]
    return pl.pallas_call(
        functools.partial(back_kernel, half=half, P_=P_, PP=PP),
        grid=(nb // 2,), in_specs=in_specs, out_specs=out_specs, out_shape=outs,
        scratch_shapes=scratch + [pltpu.VMEM((2, images, S), F32), pltpu.VMEM((4 * PP, K + 256), BF16), pltpu.VMEM((4 * PP, K), F32),
                        pltpu.VMEM((2, width, S), F32), pltpu.VMEM((2 * width, S), BF16), pltpu.VMEM((4, PP, 2 * width), BF16),
                        pltpu.VMEM((8, K), F32), pltpu.VMEM((4 * PP, 2 * width), F32), pltpu.VMEM((width, S), F32),
                        pltpu.VMEM((width, S), F32)],
        input_output_aliases={len(args) - 1: 0} if half else {},
        compiler_params=pltpu.CompilerParams(vmem_limit_bytes=LIMIT * 24 // 60),
        cost_estimate=cost(1),
        name="token_backward",
    )(*args)


def finish_kernel(t0, t1, t2, t3, s0, s1, s2, s3, u, tok, out, mr, sums, *, skip):
    nb, width, S = tok.shape
    first = pl.program_id(0) * nb

    @pl.when(pl.program_id(0) == 0)
    def _():
        join_stats((t0, t1, t2, t3), mr, width)
        total = ((s0[...].astype(F32) + s1[...].astype(F32)) + (s2[...].astype(F32) + s3[...].astype(F32))) * (1.0 / (4 * width))
        images = sums.shape[1]
        for i in range(2):
            sums[i] = total[skip + i * images:skip + (i + 1) * images, 0:S]

    for b in range(nb):
        at_ = pl.ds(first + b, 1)
        r = mr[1, at_, :]
        n = (tok[b].astype(F32) - mr[0, at_, :]) * r
        out[b] = u[b] - r * (sums[0, at_, :] + n * sums[1, at_, :])


def finish_call(stats, sums, u, tok, skip, steps=4):
    images, width, S = tok.shape
    part = pl.BlockSpec((images // steps, width, S), lambda i: (i, 0, 0))
    return pl.pallas_call(
        functools.partial(finish_kernel, skip=skip),
        grid=(steps,),
        in_specs=[whole(stats[0].shape)] * 4 + [whole(sums[0].shape)] * 4 + [part, part],
        out_specs=part,
        out_shape=shape((images, width, S)),
        scratch_shapes=[pltpu.VMEM((2, images, S), F32), pltpu.VMEM((2, images, S), F32)],
        compiler_params=pltpu.CompilerParams(vmem_limit_bytes=LIMIT * 24 // 60),
        cost_estimate=cost(0),
        name="norm_backward",
    )(*stats, *sums, u, tok)


def masks_of(dp):
    return [6, 2, 1] if dp == 8 else [1 << k for k in reversed(range(dp.bit_length() - 1))]


def dp_place(rel, dp):
    return rel ^ ((rel >> 1) & 2) if dp == 8 else rel


UNITS = 6
GROUPS = 3


def orders(dims):
    last, *most = dims
    if len(dims) == 4:
        a, x, y = most
        most = [x, y, a]
    return [(*most[g % len(most):], *most[:g % len(most)], last) for g in range(GROUPS)]


def first_kernel(k4, r4, k3, r3, *outs, plans):
    dp, _, blk, W = k4.shape
    n = 2 * dp
    bits = n.bit_length() - 1
    unit = 2 * W // UNITS
    per = UNITS // GROUPS
    for g, plan in enumerate(plans):
        for i in range(n):
            coord = [(i >> (bits - 1 - d)) & 1 for d in plan]
            j = 0
            for v in coord[1:]:
                j = 2 * j + v
            for m in range(per):
                k, r = (k4, r4) if g * per + m < UNITS // 2 else (k3, r3)
                c = pl.ds((g * per + m) % (UNITS // 2) * unit, unit)
                v = k[i // 2, i % 2, :, c].astype(F32) + r[i // 2, i % 2, :, c].astype(F32)
                outs[g + GROUPS * coord[0]][j, :, m * unit:(m + 1) * unit] = v.astype(BF16)


def next_kernel(*refs):
    ins, outs = refs[:2 * GROUPS], refs[2 * GROUPS:]
    for g in range(GROUPS):
        k, r = ins[2 * g], ins[2 * g + 1]
        n = k.shape[0] // 2
        outs[g][...] = (k[0:n].astype(F32) + r[0:n].astype(F32)).astype(BF16)
        v = (k[n:].astype(F32) + r[n:].astype(F32)).astype(BF16)
        if n > 1:
            outs[GROUPS + g][...] = v
        else:
            outs[GROUPS][g] = v[0]


def last_kernel(*refs):
    ins, got, outs = refs[:GROUPS], refs[GROUPS], refs[GROUPS + 1:]
    unit = 2 * outs[0].shape[1] // UNITS
    per = UNITS // GROUPS
    for g in range(GROUPS):
        v = ins[g][0].astype(F32) + got[g].astype(F32)
        for m in range(per):
            u = g * per + m
            outs[u // (UNITS // 2)][:, u % (UNITS // 2) * unit:(u % (UNITS // 2) + 1) * unit] = v[:, m * unit:(m + 1) * unit]


def plain_call(kernel, args, outs, name, weight=0):
    return pl.pallas_call(
        kernel, grid=(1,), in_specs=[whole(a.shape) for a in args], out_specs=[whole(o.shape) for o in outs], out_shape=outs,
        compiler_params=pltpu.CompilerParams(vmem_limit_bytes=LIMIT * 24 // 60), name=name, cost_estimate=cost(weight))(*args)


def swap(v, mask, world):
    return lax.ppermute(v, ("dp", "chan"), [(i, i ^ mask) for i in range(world)])


def after(values, done):
    *values, _ = lax.optimization_barrier((*values, done))
    return values


def start_sums(keep4, send4, keep3, send3):
    dp, _, blk, W = keep4.shape
    plans = orders(list(range(len(masks_of(dp)) + 1)))
    return plain_call(functools.partial(first_kernel, plans=plans), (keep4, swap(send4, 1, dp * 4), keep3, swap(send3, 1, dp * 4)),
                      [shape((dp, blk, 2 * W // GROUPS), BF16)] * (2 * GROUPS), "sum_first")


def send_step(parts, t, dp):
    masks = [4 * m for m in masks_of(dp)] + [2]
    plans = orders(list(range(len(masks))))
    return [*parts[:GROUPS], *(swap(v, masks[plans[g][t]], dp * 4) for g, v in enumerate(parts[GROUPS:]))]


def sum_step(got):
    n, blk, cols = got[0].shape
    if n == 1:
        return plain_call(last_kernel, got, [shape((blk, GROUPS * cols // 2))] * 2, "sum_last")
    sends = [shape((n // 2, blk, cols), BF16)] * GROUPS if n > 2 else [shape((GROUPS, blk, cols), BF16)]
    got = [v for g in range(GROUPS) for v in (got[g], got[GROUPS + g])]
    return plain_call(next_kernel, got, [shape((n // 2, blk, cols), BF16)] * GROUPS + sends, "sum_next")


def join_terms(s, PP):
    v = s[2 * PP:2 * PP + VEC] + s[2 * PP + VEC:2 * PP + 2 * VEC]
    hi = v.astype(BF16).astype(F32)
    return jnp.concatenate([s[0:2 * PP], hi, v - hi], axis=0).astype(BF16)


def quarter_sum_kernel(*refs, PP):
    *ins, out = refs
    v = [q[...].astype(F32) for q in ins]
    out[...] = join_terms((v[0] + v[1]) + (v[2] + v[3]) if len(v) == 4 else v[0] + v[1], PP)


def quarter_sum(ins, PP):
    dims = (2 * PP + 2 * VEC, ins[0].shape[1])
    return plain_call(functools.partial(quarter_sum_kernel, PP=PP), ins, [shape(dims, BF16)], "quarter_sum")[0]


def unpack_kernel(ids, q0, q1, q2, q3, w1, w2, b3, g2, c2, b4, b1, b2, g1, c1, quarters, vec, *, P_, PP):
    K = w1.shape[1]
    for k, q in enumerate((q0, q1, q2, q3)):
        quarters[ids[1] ^ k] = q[...]
    for j in range(4):
        s = quarters[j].astype(F32)
        w1[j * P_:(j + 1) * P_, :] = s[0:P_]
        w2[j * P_:(j + 1) * P_, :] = s[PP:PP + P_]
        vec[j * VEC:(j + 1) * VEC, :] = s[2 * PP:2 * PP + VEC] + s[2 * PP + VEC:2 * PP + 2 * VEC]
    row = 0
    for o in (b3, g2, c2, b4):
        for r in range(o.shape[0] // K):
            o[r * K:(r + 1) * K] = vec[row]
            row += 1
    b1[...] = vec[row]
    v = vec[row + 1:row + 2, :]
    b2[...] = jnp.concatenate([v[:, j * PP:j * PP + P_] for j in range(4)], axis=1)[0]
    row += 2
    for o in (g1, c1):
        for r in range(2):
            o[r * K:(r + 1) * K] = vec[row]
            row += 1


def unpack_call(ids, quarters, S, F, W, P_, PP):
    dims = quarters[0].shape
    K = dims[1]
    outs = [(S, K), (S, K), (F,), (W,), (W,), (W,), (K,), (S,), (W,), (W,)]
    return pl.pallas_call(
        functools.partial(unpack_kernel, P_=P_, PP=PP), grid=(1,),
        in_specs=[SMEM] + [whole(dims)] * 4, out_specs=[whole(o) for o in outs], out_shape=[shape(o) for o in outs],
        scratch_shapes=[pltpu.VMEM((4,) + dims, BF16), pltpu.VMEM((4 * VEC, K), F32)],
        compiler_params=pltpu.CompilerParams(vmem_limit_bytes=LIMIT * 8 // 60), name="unpack", cost_estimate=cost(0))(ids, *quarters)


def exchange(value):
    return [value] + [lax.ppermute(value, "chan", [(i, i ^ k) for i in range(4)]) for k in (1, 2, 3)]


def trade(pieces):
    return [pieces[0]] + [lax.ppermute(pieces[k], "chan", [(i, i ^ k) for i in range(4)]) for k in (1, 2, 3)]


def shards(tokens, ln1_gain, ln1_bias, mix_in, mix_in_bias, mix_out, mix_out_bias, ln2_gain, ln2_bias,
           chan_in, chan_in_bias, chan_out, chan_out_bias, skip_masks, cotangent):
    images, S, width = tokens.shape
    P_ = cotangent.shape[1]
    W = cotangent.shape[2]
    PP = -(-P_ // 8) * 8
    tok = jnp.swapaxes(tokens, 1, 2)
    w_outT = jnp.swapaxes(mix_out, 0, 1)
    row = lambda v: v.reshape(1, -1)
    chan = lax.axis_index("chan")
    keep1 = skip_masks[:, 0].astype(F32)
    keep2 = skip_masks[:, 1].astype(F32)
    g1, c1 = row(ln1_gain), row(ln1_bias)

    stats = exchange(stats_call(tok))
    halves = (0, 1)
    dp = lax.axis_size("dp")
    ids = jnp.stack([lax.axis_index("dp"), chan]).astype(jnp.int32)
    R = -(-(images // 2) * P_ // 16) * 16
    og, sum_b4 = upstream_call(keep2, cotangent, R)
    fwd = [token_call(ids, keep1, stats, tok, mix_in, row(mix_in_bias), w_outT, row(mix_out_bias), g1, c1, h, P_, PP) for h in halves]
    arrived = [trade(f) for f in fwd]
    weights = (chan_in, chan_out, row(chan_in_bias), row(chan_out_bias), row(ln2_gain), row(ln2_bias))
    c0 = chan_call(ids, keep2, arrived[0], cotangent, og, 0, *weights, None, dp)
    part4, part3, b3_0, out = c0[:4]
    c1_ = chan_call(ids, keep2, arrived[1], cotangent, og, 1, *weights, (part4, part3, out), dp)
    keep4, send4, keep3, send3, b3_1, out = c1_[:6]
    tails = (c0[4:], c1_[6:])
    returned = [trade(t[:4]) for t in tails]
    vecs = [b3_0, b3_1, tails[0][4], tails[1][4], tails[0][5], tails[1][5], sum_b4]
    tokens_back = functools.partial(back_call, ids, keep1, stats)
    u, *sums = tokens_back(returned[0], tok, mix_in, row(mix_in_bias), w_outT, g1, c1, 0, P_, PP, None, None, None)
    keep4, keep3 = after((keep4, keep3), u)
    parts = list(start_sums(keep4, send4, keep3, send3))
    pairs = send_step(parts, 0, dp)
    u, = after((u,), parts[0])
    u, *pieces = tokens_back(returned[1], tok, mix_in, row(mix_in_bias), w_outT, g1, c1, 1, P_, PP, [*sums[1:], sums[0]], vecs, u)
    pieces = trade(pieces)
    quarter = quarter_sum(pieces, PP)
    masks = [4 * m for m in reversed(masks_of(dp))]
    grad = None
    for t, mask in enumerate(masks):
        other = swap(quarter, mask, dp * 4)
        parts = sum_step(after(pairs, quarter))
        pairs = send_step(parts, t + 1, dp)
        done = parts[0]
        if grad is None:
            done = grad = finish_call(stats, after(pieces, done), u, tok, 2 * PP + 2 * VEC)
        quarter = quarter_sum(after((quarter, other), done), PP)
    share_w4, share_w3 = sum_step(after(pairs, quarter))
    s_w1, s_w2, s_b3, s_g2, s_c2, s_b4, s_b1, s_b2, s_g1, s_c1 = unpack_call(
        ids, exchange(quarter), S, chan_in.shape[1], W, P_, PP)
    return (out, jnp.swapaxes(grad, 1, 2), s_g1, s_c1, s_w1, s_b1, jnp.swapaxes(s_w2, 0, 1), s_b2, s_g2, s_c2,
            jnp.swapaxes(share_w3, 0, 1), s_b3, share_w4, s_b4)


def solution(mesh):
    rep = P()
    return jax.shard_map(
        shards, mesh=mesh,
        in_specs=(P("dp", None, "chan"), P("chan"), P("chan")) + (rep,) * 10 + (P("dp", None), P("dp", "chan", None)),
        out_specs=(P("dp", "chan", None), P("dp", None, "chan"), rep, rep, rep, rep, rep, rep, rep, rep,
                   P(None, ("dp", "chan")), rep, P(("dp", "chan"), None), rep),
        check_vma=False,
    )
```
